32 devices in a mesh: req: 8 (over z, y), tensor: 4 (over x, core).
Axes of the slice: x: 2, y: 2, z: 4, core: 2. Of those that a mesh axis runs over, the one named last changes fastest.
Arguments:
- hidden: bfloat16 [192, 16384], P('tensor', 'req'), may hold values from -6 to 6
- w_query: bfloat16 [16384, 8192], P('req', 'tensor'), may hold values from -0.046875 to 0.046875
- keyvalue_weight: bfloat16 [16384, 1024], P('req', 'tensor'), may hold values from -0.125 to 0.125
- w_out: bfloat16 [8192, 16384], P('tensor', 'req'), may hold values from -0.25 to 0.25
- keyvalue_cache: bfloat16 [8, 4096, 1024], P('req', 'tensor'), may hold values from -260 to 260
- cache_live: int32 [8, 256], P('req'), may hold values 0 or 1
- tree_size: int32 [8], replicated, may hold values from 1 to 48, 192 in all
- tree_parent: int32 [8, 48], replicated, may hold values from 0 to 46, as said below
- slot_request: int32 [8], replicated, may hold values from 0 to 7, each once
Outputs:
- mixed: bfloat16 [192, 16384], P('tensor', 'req')
The draws below stay inside these ranges and needn't reach their ends.
Inputs may be any that keep to these rules, and one draw needn't show every extreme that they name: `tree_size`: the sizes add up to 192, and the largest is exactly 48. `tree_parent`: for node k >= 1 of a request's tree the parent is one of the nodes max(0, k - 4) .. k - 1; the entry of node 0, the root, is 0. Entries of nodes at or beyond the request's tree_size are present but belong to no node. `slot_request`: A permutation of the requests.
All inputs are finite; a program needn't handle non-finite values. No bound on the sum of `cache_live` on one device may be relied on, other than what follows from the above.
Results may differ from the reference program's by a relative error of at most 0.04.
Values may be sent and summed in bfloat16 or wider, within the bound.
A program may use at most 128 MiB of HBM per device.

```python
import math
import jax
import jax.numpy as jnp
import numpy as np
from jax import lax

MODEL_WIDTH = 16384
HEAD_SIZE = 128
QUERY_HEADS = 64
KEYVALUE_HEADS = 4
MOST_TREE_NODES = 48
CACHE_POSITIONS = 4096
CBLK = 16
REQS = 8
ROWS = 192
NBLK = 256
N_REQ = 8
N_TENSOR = 4


def draw_keyvalue_cache(key, part):
    packed_row_width = 2 * KEYVALUE_HEADS * HEAD_SIZE
    base_key = jax.random.fold_in(key, 0)
    return jnp.clip(jax.random.normal(base_key, (REQS, CACHE_POSITIONS, packed_row_width), jnp.float32), -6.0, 6.0).astype(jnp.bfloat16)


def draw_tree_parent(key, part):
    node_ids = jnp.arange(MOST_TREE_NODES, dtype=jnp.int32)
    request_ids = jnp.arange(REQS, dtype=jnp.int32)
    reach_back = jnp.broadcast_to(jnp.maximum(jnp.minimum(node_ids, 4), 1), (REQS, MOST_TREE_NODES))
    step_back = jax.random.randint(key, (REQS, MOST_TREE_NODES), 0, reach_back, dtype=jnp.int32)
    forced = (request_ids[:, None] == 0) & (node_ids[None, :] == MOST_TREE_NODES - 1)
    step_back = jnp.where(forced, 0, step_back)
    return jnp.maximum(node_ids[None, :] - 1 - step_back, 0).astype(jnp.int32)


def plant(entries, key, low, top_value):
    spot = [jax.random.randint(jax.random.fold_in(key, axis), (), 0, length) for axis, length in enumerate(entries.shape)]
    main_axis = entries.shape.index(max(entries.shape))
    beside = spot[:main_axis] + [(spot[main_axis] + 1) % entries.shape[main_axis]] + spot[main_axis + 1:]
    return entries.at[tuple(spot)].set(low).at[tuple(beside)].set(top_value)


def shard_levels(own_key, shape, cuts, least, high):
    loudness, own = 1.0, jax.random.fold_in(own_key, 6)
    for position, shards_of in cuts:
        draws = jnp.exp(jax.random.uniform(jax.random.fold_in(own, position), (shards_of,), jnp.float32, least / len(cuts), high / len(cuts)))
        loudness = loudness * jnp.repeat(draws, shape[position] // shards_of).reshape([-1 if axis == position else 1 for axis in range(len(shape))])
    return loudness


def length_profile(number_of, total, bound, slope):
    loads = [(1 << 20) // math.isqrt(grade ** slope) + 1 for grade in range(2, number_of + 1)]
    surplus, holding = total - bound - (number_of - 1), [1] * (number_of - 1)
    while surplus > 0:
        movable = [i for i in range(number_of - 1) if holding[i] < bound]
        mass, remaining = sum([loads[i] for i in movable]), surplus
        for i in movable:
            extra = min(bound - holding[i], max(1, remaining * loads[i] // mass), surplus)
            holding[i] = holding[i] + extra
            surplus = surplus - extra
    return np.array([bound] + holding)


def ragged(rng, count, total, most, skew):
    if count == 2:
        one = jax.random.randint(rng, (), max(1, total - most), min(most, total - 1) + 1)
        return jnp.stack([one, total - one])
    tallies = jnp.asarray(length_profile(count, total, most, skew), jnp.int32)
    pairs = (count - 1) // 2
    giver, taker = tallies[1:1 + 2 * pairs:2], tallies[2:2 + 2 * pairs:2]
    room = jnp.minimum(giver - 1, most - taker)
    passed = jax.random.randint(jax.random.fold_in(rng, 1), (pairs,), 0, 1 << 20) % (room + 1)
    tallies = tallies.at[1:1 + 2 * pairs:2].set(giver - passed).at[2:2 + 2 * pairs:2].set(taker + passed)
    return tallies[jax.random.permutation(jax.random.fold_in(rng, 2), count)]


def noise(stream_key, shape, width, reach, pieces=(), kind=jnp.bfloat16):
    drawn = width * jax.random.normal(stream_key, shape, jnp.float32)
    if pieces:
        drawn = drawn * shard_levels(stream_key, shape, pieces, -0.22, 0.18)
    return jnp.clip(drawn, -reach, reach).astype(kind)


def setup_inputs(seed: int = 0) -> dict:
    streams_of = jax.random.split(jax.random.key(seed), 10)
    return {
        "hidden": noise(streams_of[0], (ROWS, MODEL_WIDTH), 1.0, 6.0, ((0, 4), (1, 8))),
        "w_query": noise(streams_of[1], (MODEL_WIDTH, QUERY_HEADS * HEAD_SIZE), MODEL_WIDTH ** -0.5, 0.046875, ((0, 8), (1, 4))),
        "keyvalue_weight": noise(streams_of[2], (MODEL_WIDTH, 2 * KEYVALUE_HEADS * HEAD_SIZE), (MODEL_WIDTH // 8) ** -0.5, 0.125, ((0, 8), (1, 4))),
        "w_out": noise(streams_of[3], (QUERY_HEADS * HEAD_SIZE, MODEL_WIDTH), (QUERY_HEADS * HEAD_SIZE // 16) ** -0.5, 0.25, ((0, 4), (1, 8))),
        "keyvalue_cache": draw_keyvalue_cache(jax.random.fold_in(streams_of[9], 71), 0),
        "cache_live": plant((jax.random.randint(streams_of[5], (REQS, NBLK), 0, 2) < 1).astype(jnp.int32), jax.random.fold_in(streams_of[5], 1), 0, 1),
        "tree_size": ragged(streams_of[6], REQS, ROWS, MOST_TREE_NODES, 2).astype(jnp.int32),
        "tree_parent": draw_tree_parent(jax.random.fold_in(streams_of[9], 71), 0),
        "slot_request": jax.random.permutation(streams_of[8], REQS).astype(jnp.int32),
    }


ROPE_BASE = 500000.0
NEGATIVE = -1e+30

def rounded(values):
    return lax.optimization_barrier(values.astype(jnp.bfloat16))

def ancestors(parents):
    node_ids = jnp.arange(MOST_TREE_NODES, dtype=jnp.int32)
    linked = (parents[..., :, None] == node_ids).astype(jnp.float32)
    identity = (node_ids[:, None] == node_ids[None, :]).astype(jnp.float32)
    closure = jnp.maximum(linked, identity)
    for sweep in range((MOST_TREE_NODES - 1).bit_length()):
        closure = jnp.minimum(jnp.matmul(closure, closure, precision=lax.Precision.HIGHEST), 1.0)
    return closure

def rotary(tree_depth):
    half_ids = jnp.arange(HEAD_SIZE // 2, dtype=jnp.float32)
    inv_freq = 1.0 / ROPE_BASE ** (half_ids * 2.0 / HEAD_SIZE)
    angles = (tree_depth + CACHE_POSITIONS)[..., None] * inv_freq
    angles = jnp.concatenate([angles, angles], axis=-1)
    return (jnp.cos(angles), jnp.sin(angles))

def rotate(values, cosine_table, sine_table):
    widened = values.astype(jnp.float32)
    lower_half, upper_half = jnp.split(widened, 2, axis=-1)
    turned = jnp.concatenate([-upper_half, lower_half], axis=-1)
    return widened * cosine_table[..., None, :] + turned * sine_table[..., None, :]

def reference(hidden, w_query, keyvalue_weight, w_out, keyvalue_cache, cache_live, tree_size, tree_parent, slot_request):
    row_total = hidden.shape[0]
    request_total = tree_size.shape[0]
    query_columns = QUERY_HEADS * HEAD_SIZE
    query_group_size = QUERY_HEADS // KEYVALUE_HEADS
    score_scale = 1.0 / math.sqrt(HEAD_SIZE)
    width_block = MODEL_WIDTH // N_REQ
    w_both = jnp.concatenate([w_query, keyvalue_weight], axis=1)
    summed = jnp.zeros((row_total, w_both.shape[1]), jnp.float32)
    for block_index in range(N_REQ):
        lower_col = block_index * width_block
        partial_sum = jnp.dot(hidden[:, lower_col:lower_col + width_block], w_both[lower_col:lower_col + width_block], preferred_element_type=jnp.float32)
        summed = summed + rounded(partial_sum).astype(jnp.float32)
    projected = rounded(summed)
    row_ends = jnp.cumsum(tree_size).astype(jnp.int32)
    starts = (row_ends - tree_size).astype(jnp.int32)
    request_ids = jnp.arange(request_total, dtype=jnp.int32)
    home_slot = lax.optimization_barrier(jnp.sum(jnp.where(slot_request[None, :] == request_ids[:, None], request_ids[None, :], 0), axis=1)).astype(jnp.int32)
    node_ids = jnp.arange(MOST_TREE_NODES, dtype=jnp.int32)

    def attend(request):
        row_ids = jnp.minimum(starts[request] + node_ids, row_total - 1).astype(jnp.int32)
        is_valid = node_ids < tree_size[request]
        occupied_rows = jnp.take(projected, row_ids, axis=0)
        occupied_rows = jnp.where(is_valid[:, None], occupied_rows, jnp.zeros_like(occupied_rows))
        queries = occupied_rows[:, :query_columns].reshape(MOST_TREE_NODES, QUERY_HEADS, HEAD_SIZE)
        draft_tree_keyvalue = occupied_rows[:, query_columns:].reshape(MOST_TREE_NODES, 2, HEAD_SIZE, KEYVALUE_HEADS)
        draft_keys = jnp.transpose(draft_tree_keyvalue[:, 0], (0, 2, 1))
        draft_values = jnp.transpose(draft_tree_keyvalue[:, 1], (0, 2, 1))
        closure = ancestors(tree_parent[request])
        tree_depth = lax.optimization_barrier(jnp.sum(closure, axis=-1)) - 1.0
        cosine_table, sine_table = rotary(tree_depth)
        rotated_query = rounded(rotate(queries, cosine_table, sine_table)).astype(jnp.float32)
        key_rot = rounded(rotate(draft_keys, cosine_table, sine_table)).astype(jnp.float32)
        tree_values = draft_values.astype(jnp.float32)
        cache_position_slot = home_slot[request]
        cached_row_block = keyvalue_cache[cache_position_slot].reshape(CACHE_POSITIONS, KEYVALUE_HEADS, 2, HEAD_SIZE).astype(jnp.float32)
        live_mask = jnp.repeat(cache_live[cache_position_slot], CBLK) > 0
        grouped_queries = rotated_query.reshape(MOST_TREE_NODES, KEYVALUE_HEADS, query_group_size, HEAD_SIZE)
        cache_scores = jnp.einsum('kgjd,pgd->kgjp', grouped_queries, cached_row_block[:, :, 0]) * score_scale
        tree_scores = jnp.einsum('kgjd,igd->kgji', grouped_queries, key_rot) * score_scale
        cache_ok = live_mask[None, None, None, :]
        tree_ok = (closure > 0.5)[:, None, None, :]
        top_score = jnp.maximum(lax.optimization_barrier(jnp.max(jnp.where(cache_ok, cache_scores, NEGATIVE), axis=-1)), lax.optimization_barrier(jnp.max(jnp.where(tree_ok, tree_scores, NEGATIVE), axis=-1)))
        cache_weights = jnp.where(cache_ok, jnp.exp(cache_scores - top_score[..., None]), 0.0)
        tree_weights = jnp.where(tree_ok, jnp.exp(tree_scores - top_score[..., None]), 0.0)
        weight_sum = lax.optimization_barrier(jnp.sum(cache_weights, axis=-1)) + lax.optimization_barrier(jnp.sum(tree_weights, axis=-1))
        mixed_sum = jnp.einsum('kgjp,pgd->kgjd', rounded(cache_weights).astype(jnp.float32), cached_row_block[:, :, 1])
        mixed_sum = mixed_sum + jnp.einsum('kgji,igd->kgjd', rounded(tree_weights).astype(jnp.float32), tree_values)
        return (mixed_sum / weight_sum[..., None]).reshape(MOST_TREE_NODES, query_columns).astype(jnp.bfloat16)
    attention_all = lax.map(attend, request_ids)
    row_ids = jnp.arange(row_total, dtype=jnp.int32)
    owner_req = lax.optimization_barrier(jnp.sum((row_ends[None, :] <= row_ids[:, None]).astype(jnp.int32), axis=1)).astype(jnp.int32)
    node_of_row = (row_ids - starts[owner_req]).astype(jnp.int32)
    attention_rows = attention_all[owner_req, node_of_row]
    head_block = query_columns // N_TENSOR
    summed_out = jnp.zeros((row_total, MODEL_WIDTH), jnp.float32)
    for block_index in range(N_TENSOR):
        lower_col = block_index * head_block
        partial_sum = jnp.dot(attention_rows[:, lower_col:lower_col + head_block], w_out[lower_col:lower_col + head_block], preferred_element_type=jnp.float32)
        summed_out = summed_out + rounded(partial_sum).astype(jnp.float32)
    return summed_out.astype(jnp.bfloat16)
```

```python
import functools
import math

import jax
import jax.numpy as jnp
from jax import lax
from jax.experimental import pallas as pl
from jax.experimental.pallas import tpu as pltpu
from jax.sharding import PartitionSpec as P

HEAD_SIZE = 128
QUERY_HEADS = 64
KEYVALUE_HEADS = 4
MOST_TREE_NODES = 48
CACHE_POSITIONS = 4096
CBLK = 16


ROPE_BASE = 500000.0
NEGATIVE = -1e30


def lookup(table_vals, index_vals):
    table_ids = jnp.arange(table_vals.shape[0], dtype=jnp.int32)
    return jnp.sum(
        jnp.where(index_vals[:, None] == table_ids[None, :], table_vals[None, :], 0), axis=1
    )


def ancestors(parents):
    node_ids = jnp.arange(MOST_TREE_NODES, dtype=jnp.int32)
    linked = (parents[..., :, None] == node_ids).astype(jnp.float32)
    identity = (node_ids[:, None] == node_ids[None, :]).astype(jnp.float32)
    closure = jnp.maximum(linked, identity)
    for sweep in range((MOST_TREE_NODES - 1).bit_length()):
        closure = jnp.minimum(jnp.matmul(closure, closure, precision=lax.Precision.HIGHEST), 1.0)
    return closure


def rotary(tree_depth):
    half_ids = jnp.arange(HEAD_SIZE // 2, dtype=jnp.float32)
    inv_freq = 1.0 / ROPE_BASE ** (half_ids * 2.0 / HEAD_SIZE)
    angles = (tree_depth + CACHE_POSITIONS)[..., None] * inv_freq
    angles = jnp.concatenate([angles, angles], axis=-1)
    return (jnp.cos(angles), jnp.sin(angles))


def rotate(values, cosine_table, sine_table):
    widened = values.astype(jnp.float32)
    lower_half, upper_half = jnp.split(widened, 2, axis=-1)
    turned = jnp.concatenate([-upper_half, lower_half], axis=-1)
    return widened * cosine_table[..., None, :] + turned * sine_table[..., None, :]


MESH = pl.DeviceIdType.MESH
VMEM_BYTES = 56 * 1024 * 1024


def inner_of(count):
    inner = 1
    while inner * inner * 4 <= count:
        inner *= 2
    return inner


def target(axis, index):
    other = "tensor" if axis == "req" else "req"
    return {axis: index, other: lax.axis_index(other)}


def place(axis, inner):
    count = lax.axis_size(axis)
    me = lax.axis_index(axis)
    outer = count // inner
    major, minor = me // inner, lax.rem(me, inner)

    def at(step_major, step_minor):
        return lax.rem(major + step_major + outer, outer) * inner + lax.rem(
            minor + step_minor + inner, inner
        )

    return outer, at


def greet(axes):
    barrier = pltpu.get_barrier_semaphore()
    greeted = 0
    for axis, inner in axes:
        outer, at = place(axis, inner)
        steps = [(d, 0) for d in range(1, outer)] + [(0, e) for e in range(1, inner)]
        for d, e in steps:
            pl.semaphore_signal(
                barrier, inc=1, device_id=target(axis, at(d, e)), device_id_type=MESH
            )
            greeted += 1
    pl.semaphore_wait(barrier, greeted)


def remote(source, landing, sends, recvs, slot, axis, index):
    return pltpu.make_async_remote_copy(
        src_ref=source,
        dst_ref=landing,
        send_sem=sends.at[slot],
        recv_sem=recvs.at[slot],
        device_id=target(axis, index),
        device_id_type=MESH,
    )


def start_gather(axis, inner, own, part, sends, recvs):
    outer, at = place(axis, inner)
    started = []
    for d in range(1, outer):
        copy = remote(own, part(at(0, 0)), sends, recvs, d, axis, at(d, 0))
        copy.start()
        started.append(copy)
    for e in range(1, inner):
        copy = remote(own, part(at(0, 0)), sends, recvs, e * outer, axis, at(0, e))
        copy.start()
        started.append(copy)
    return started


def finish_gather(axis, inner, own, part, sends, recvs, started):
    outer, at = place(axis, inner)
    for d in range(1, outer):
        landed = part(at(-d, 0))
        remote(own, landed, sends, recvs, d, axis, at(d, 0)).wait_recv()
        for e in range(1, inner):
            copy = remote(landed, landed, sends, recvs, e * outer + d, axis, at(0, e))
            copy.start()
            started.append(copy)
    for e in range(1, inner):
        for d in range(outer):
            landed = part(at(-d, -e))
            remote(own, landed, sends, recvs, e * outer + d, axis, at(0, e)).wait_recv()
    for copy in started:
        copy.wait_send()


def sum_scatter(axis, inner, produce, part, near, staged, far, sends, recvs, finish):
    outer, at = place(axis, inner)
    order = list(range(1, outer)) + [0]
    started = []
    for d in order:
        for e in range(1, inner):
            index = at(d, e)
            produce(index)
            copy = remote(
                part(index),
                near.at[(e - 1) * outer + d],
                sends,
                recvs,
                e * outer + d,
                axis,
                at(0, e),
            )
            copy.start()
            started.append(copy)
    for d in order:
        produce(at(d, 0))
    total = None
    for d in order:
        block = part(at(d, 0))
        total = block[...].astype(jnp.float32)
        for e in range(1, inner):
            slot = (e - 1) * outer + d
            remote(
                block, near.at[slot], sends, recvs, e * outer + d, axis, at(0, e)
            ).wait_recv()
            total = total + near[slot].astype(jnp.float32)
        if d:
            staged[d - 1] = total.astype(jnp.bfloat16)
            copy = remote(
                staged.at[d - 1], far.at[d - 1], sends, recvs, d, axis, at(d, 0)
            )
            copy.start()
            started.append(copy)
    for d in range(1, outer):
        remote(
            staged.at[d - 1], far.at[d - 1], sends, recvs, d, axis, at(d, 0)
        ).wait_recv()
        total = total + far[d - 1].astype(jnp.float32)
    finish(total.astype(jnp.bfloat16))
    for copy in started:
        copy.wait_send()


def tiles(width):
    step = 256 if width % 256 == 0 else width
    return width // step, step


def project_kernel(
    req_inner,
    core_inner,
    group_size,
    hidden_ref,
    pick_ref,
    wq_ref,
    wkv_ref,
    cache_ref,
    query_ref,
    kv_ref,
    kvcache_ref,
    rows,
    wq,
    wkv,
    product,
    blocks,
    near,
    staged,
    far,
    load_sem,
    row_send,
    row_recv,
    cache_send,
    cache_recv,
    sum_send,
    sum_recv,
    kv_send,
    kv_recv,
):
    tensor_count = lax.axis_size("tensor")
    me = lax.axis_index("tensor")
    rows_here = hidden_ref.shape[0]
    query_columns = wq.shape[1]
    heads_here = query_columns // HEAD_SIZE
    pair = 2 * HEAD_SIZE
    positions = cache_ref.shape[0]
    load_q = pltpu.make_async_copy(wq_ref, wq, load_sem.at[0])
    load_kv = pltpu.make_async_copy(wkv_ref, wkv, load_sem.at[1])
    load_q.start()
    load_kv.start()
    greet([("tensor", tensor_count), ("req", req_inner)])

    def row_part(index):
        return rows.at[pl.ds(pl.multiple_of(index * rows_here, rows_here), rows_here)]

    started = start_gather("tensor", core_inner, hidden_ref, row_part, row_send, row_recv)
    rows[pl.ds(pl.multiple_of(me * rows_here, rows_here), rows_here), :] = hidden_ref[...]
    finish_gather("tensor", core_inner, hidden_ref, row_part, row_send, row_recv, started)

    def cache_part(owner, reader):
        head = reader * heads_here // group_size
        return (
            cache_ref.at[:, pl.ds(pl.multiple_of(head * pair, pair), pair)],
            kvcache_ref.at[pl.ds(pl.multiple_of(owner * positions, positions), positions)],
        )

    source, landing = cache_part(me, me)
    own_cache = pltpu.make_async_copy(source, landing, load_sem.at[2])
    own_cache.start()
    cache_copies = []
    for step in range(1, tensor_count):
        reader = lax.rem(me + step, tensor_count)
        source, landing = cache_part(me, reader)
        copy = remote(source, landing, cache_send, cache_recv, step, "tensor", reader)
        copy.start()
        cache_copies.append(copy)

    load_q.wait()
    load_kv.wait()
    steps, step_width = tiles(query_columns)

    @pl.loop(0, steps)
    def _(step):
        columns = pl.ds(pl.multiple_of(step * step_width, step_width), step_width)
        product[:, columns] = jnp.dot(
            rows[...], wq[:, columns], preferred_element_type=jnp.float32
        ).astype(jnp.bfloat16)

    product[:, query_columns:] = jnp.dot(
        rows[...], wkv[...], preferred_element_type=jnp.float32
    ).astype(jnp.bfloat16)

    def slot_rows(index):
        return pl.ds(pl.multiple_of(index * MOST_TREE_NODES, MOST_TREE_NODES), MOST_TREE_NODES)

    def produce(index):
        blocks[slot_rows(index), :] = jnp.dot(
            pick_ref[slot_rows(index), :], product[...], preferred_element_type=jnp.float32
        ).astype(jnp.bfloat16)

    def finish(total):
        query_ref[...] = total[:, :query_columns]
        kv_ref[me] = total[:, query_columns:]

    sum_scatter(
        "req",
        req_inner,
        produce,
        lambda index: blocks.at[slot_rows(index)],
        near,
        staged,
        far,
        sum_send,
        sum_recv,
        finish,
    )
    own_kv = kv_ref.at[me]
    started = start_gather(
        "tensor", tensor_count, own_kv, lambda index: kv_ref.at[index], kv_send, kv_recv
    )
    finish_gather(
        "tensor", tensor_count, own_kv, lambda index: kv_ref.at[index], kv_send, kv_recv, started
    )
    own_cache.wait()
    for step in range(1, tensor_count):
        owner = lax.rem(me - step + tensor_count, tensor_count)
        source, landing = cache_part(owner, me)
        remote(source, landing, cache_send, cache_recv, step, "tensor", owner).wait_recv()
    for copy in cache_copies:
        copy.wait_send()


def project(hidden, pick, w_query, keyvalue_weight, cache):
    tensor_count, req_count = lax.axis_size("tensor"), lax.axis_size("req")
    req_inner, core_inner = inner_of(req_count), 2
    rows_here, width = hidden.shape
    query_columns, kv_columns = w_query.shape[1], keyvalue_weight.shape[1]
    both = query_columns + kv_columns
    outer = req_count // req_inner
    bf16, dma = jnp.bfloat16, pltpu.SemaphoreType.DMA
    any_space, vmem = pl.BlockSpec(memory_space=pl.ANY), pl.BlockSpec(memory_space=pltpu.VMEM)
    return pl.pallas_call(
        functools.partial(
            project_kernel, req_inner, core_inner, QUERY_HEADS // KEYVALUE_HEADS
        ),
        out_shape=(
            jax.ShapeDtypeStruct((MOST_TREE_NODES, query_columns), bf16),
            jax.ShapeDtypeStruct((tensor_count, MOST_TREE_NODES, kv_columns), bf16),
            jax.ShapeDtypeStruct((cache.shape[0] * tensor_count, 2 * HEAD_SIZE), bf16),
        ),
        in_specs=[vmem, vmem, any_space, any_space, any_space],
        out_specs=(vmem, vmem, any_space),
        scratch_shapes=[
            pltpu.VMEM((rows_here * tensor_count, width), bf16),
            pltpu.VMEM(w_query.shape, bf16),
            pltpu.VMEM(keyvalue_weight.shape, bf16),
            pltpu.VMEM((rows_here * tensor_count, both), bf16),
            pltpu.VMEM((req_count * MOST_TREE_NODES, both), bf16),
            pltpu.VMEM(((req_inner - 1) * outer, MOST_TREE_NODES, both), bf16),
            pltpu.VMEM((outer - 1, MOST_TREE_NODES, both), bf16),
            pltpu.VMEM((outer - 1, MOST_TREE_NODES, both), bf16),
            dma((3,)),
            dma((tensor_count,)),
            dma((tensor_count,)),
            dma((tensor_count,)),
            dma((tensor_count,)),
            dma((req_count,)),
            dma((req_count,)),
            dma((tensor_count,)),
            dma((tensor_count,)),
        ],
        compiler_params=pltpu.CompilerParams(
            collective_id=0, has_side_effects=True, vmem_limit_bytes=VMEM_BYTES
        ),
    )(hidden, pick, w_query, keyvalue_weight, cache)


def output_kernel(
    req_inner,
    core_inner,
    mix_ref,
    pick_ref,
    wo_ref,
    out_ref,
    wo,
    slots,
    rows,
    product,
    near,
    staged,
    far,
    load_sem,
    slot_send,
    slot_recv,
    sum_send,
    sum_recv,
):
    me = lax.axis_index("req")
    rows_here = out_ref.shape[0]
    load = pltpu.make_async_copy(wo_ref, wo, load_sem.at[0])
    load.start()
    greet([("req", req_inner), ("tensor", core_inner)])

    def slot_rows(index):
        return pl.ds(pl.multiple_of(index * MOST_TREE_NODES, MOST_TREE_NODES), MOST_TREE_NODES)

    def slot_part(index):
        return slots.at[slot_rows(index)]

    started = start_gather("req", req_inner, mix_ref, slot_part, slot_send, slot_recv)
    slots[slot_rows(me), :] = mix_ref[...]
    finish_gather("req", req_inner, mix_ref, slot_part, slot_send, slot_recv, started)
    steps, step_width = tiles(slots.shape[1])

    @pl.loop(0, steps)
    def _(step):
        columns = pl.ds(pl.multiple_of(step * step_width, step_width), step_width)
        rows[:, columns] = jnp.dot(
            pick_ref[...], slots[:, columns], preferred_element_type=jnp.float32
        ).astype(jnp.bfloat16)

    load.wait()
    out_steps, out_width = tiles(wo.shape[1])

    @pl.loop(0, out_steps)
    def _(step):
        columns = pl.ds(pl.multiple_of(step * out_width, out_width), out_width)
        product[:, columns] = jnp.dot(
            rows[...], wo[:, columns], preferred_element_type=jnp.float32
        ).astype(jnp.bfloat16)

    def finish(total):
        out_ref[...] = total

    sum_scatter(
        "tensor",
        core_inner,
        lambda index: None,
        lambda index: product.at[
            pl.ds(pl.multiple_of(index * rows_here, rows_here), rows_here)
        ],
        near,
        staged,
        far,
        sum_send,
        sum_recv,
        finish,
    )


def output(mix, pick, w_out):
    tensor_count, req_count = lax.axis_size("tensor"), lax.axis_size("req")
    req_inner, core_inner = inner_of(req_count), 2
    outer = tensor_count // core_inner
    row_total = pick.shape[0]
    rows_here = row_total // tensor_count
    depth, width = w_out.shape
    bf16, dma = jnp.bfloat16, pltpu.SemaphoreType.DMA
    any_space, vmem = pl.BlockSpec(memory_space=pl.ANY), pl.BlockSpec(memory_space=pltpu.VMEM)
    return pl.pallas_call(
        functools.partial(output_kernel, req_inner, core_inner),
        out_shape=jax.ShapeDtypeStruct((rows_here, width), bf16),
        in_specs=[vmem, vmem, any_space],
        out_specs=vmem,
        scratch_shapes=[
            pltpu.VMEM(w_out.shape, bf16),
            pltpu.VMEM((req_count * MOST_TREE_NODES, depth), bf16),
            pltpu.VMEM((row_total, depth), bf16),
            pltpu.VMEM((row_total, width), bf16),
            pltpu.VMEM(((core_inner - 1) * outer, rows_here, width), bf16),
            pltpu.VMEM((outer - 1, rows_here, width), bf16),
            pltpu.VMEM((outer - 1, rows_here, width), bf16),
            dma((1,)),
            dma((req_count,)),
            dma((req_count,)),
            dma((tensor_count,)),
            dma((tensor_count,)),
        ],
        compiler_params=pltpu.CompilerParams(
            collective_id=1, has_side_effects=True, vmem_limit_bytes=VMEM_BYTES
        ),
    )(mix, pick, w_out)


def body(
    hidden,
    w_query,
    keyvalue_weight,
    w_out,
    keyvalue_cache,
    cache_live,
    tree_size,
    tree_parent,
    slot_request,
):
    tensor_count = lax.axis_size("tensor")
    req_index = lax.axis_index("req")
    tensor_index = lax.axis_index("tensor")
    resident_requests = keyvalue_cache.shape[0]
    resident_slots = resident_requests * MOST_TREE_NODES
    row_total = hidden.shape[0] * tensor_count
    query_columns = w_query.shape[1]
    heads_here = query_columns // HEAD_SIZE
    query_group_size = QUERY_HEADS // KEYVALUE_HEADS
    score_scale = 1.0 / math.sqrt(HEAD_SIZE)
    kv_head = tensor_index * heads_here // query_group_size
    row_ends = jnp.cumsum(tree_size)
    starts = row_ends - tree_size
    request_ids = jnp.arange(tree_size.shape[0], dtype=jnp.int32)
    home_slot = jnp.sum(
        jnp.where(slot_request[None, :] == request_ids[:, None], request_ids[None, :], 0), axis=1
    )
    slot_ids = jnp.arange(resident_slots * lax.axis_size("req"), dtype=jnp.int32)
    owner_req = lookup(slot_request, slot_ids // MOST_TREE_NODES)
    node_ids = slot_ids % MOST_TREE_NODES
    is_valid = node_ids < lookup(tree_size, owner_req)
    row_ids = jnp.minimum(lookup(starts, owner_req) + node_ids, row_total - 1)
    all_rows = jnp.arange(row_total, dtype=jnp.int32)
    pick_rows = (
        (row_ids[:, None] == all_rows[None, :]) & is_valid[:, None]
    ).astype(jnp.bfloat16)
    query_here, keyval_parts, head_cache = project(
        hidden, pick_rows, w_query, keyvalue_weight, keyvalue_cache[0]
    )
    my_requests = lax.dynamic_slice_in_dim(
        slot_request, req_index * resident_requests, resident_requests
    )
    parents = jnp.sum(
        jnp.where(
            my_requests[:, None, None] == request_ids[None, :, None], tree_parent[None, :, :], 0
        ),
        axis=1,
    )
    closure = ancestors(parents)
    tree_depth = jnp.sum(closure, axis=-1) - 1.0
    cosine_table, sine_table = rotary(tree_depth.reshape(resident_slots))
    tree_ok = (closure > 0.5)[:, :, None, :]
    keyvalue_every_head = jnp.transpose(keyval_parts, (1, 0, 2))
    query_mine = rotate(
        query_here.reshape(resident_slots, heads_here, HEAD_SIZE), cosine_table, sine_table
    ).astype(jnp.bfloat16)
    query_grid = query_mine.reshape(resident_requests, MOST_TREE_NODES, heads_here, HEAD_SIZE)
    cache_keys = head_cache[None, :, :HEAD_SIZE]
    cache_values = head_cache[None, :, HEAD_SIZE:]
    top_now = jnp.full((resident_requests, MOST_TREE_NODES, heads_here), NEGATIVE, jnp.float32)
    scores = (
        jnp.einsum(
            "rkhd,rpd->rkhp", query_grid, cache_keys, preferred_element_type=jnp.float32
        )
        * score_scale
    )
    live_mask = (jnp.repeat(cache_live, CBLK, axis=1) > 0)[:, None, None, :]
    top_next = jnp.maximum(top_now, jnp.max(jnp.where(live_mask, scores, NEGATIVE), axis=-1))
    weights = jnp.where(live_mask, jnp.exp(scores - top_next[..., None]), 0.0)
    sum_next = jnp.sum(weights, axis=-1)
    mix_next = jnp.einsum(
        "rkhp,rpd->rkhd",
        weights.astype(jnp.bfloat16),
        cache_values,
        preferred_element_type=jnp.float32,
    )
    keyvalue_layout = keyvalue_every_head.reshape(resident_slots, 2, HEAD_SIZE, KEYVALUE_HEADS)
    head_kv = lax.dynamic_index_in_dim(keyvalue_layout, kv_head, axis=3, keepdims=False)
    key_mine = (
        rotate(head_kv[:, 0][:, None, :], cosine_table, sine_table)
        .astype(jnp.bfloat16)
        .reshape(resident_requests, MOST_TREE_NODES, HEAD_SIZE)
    )
    value_mine = head_kv[:, 1].reshape(resident_requests, MOST_TREE_NODES, HEAD_SIZE)
    query_block = query_mine.reshape(resident_requests, MOST_TREE_NODES, heads_here, HEAD_SIZE)
    tree_scores = (
        jnp.einsum("rkhd,rid->rkhi", query_block, key_mine, preferred_element_type=jnp.float32)
        * score_scale
    )
    top_score = jnp.maximum(top_next, jnp.max(jnp.where(tree_ok, tree_scores, NEGATIVE), axis=-1))
    rescale_cache = jnp.exp(top_next - top_score)
    tree_weights = jnp.where(tree_ok, jnp.exp(tree_scores - top_score[..., None]), 0.0)
    weight_total = sum_next * rescale_cache + jnp.sum(tree_weights, axis=-1)
    mix_total = mix_next * rescale_cache[..., None]
    mix_total = mix_total + jnp.einsum(
        "rkhi,rid->rkhd",
        tree_weights.astype(jnp.bfloat16),
        value_mine,
        preferred_element_type=jnp.float32,
    )
    attention = (
        (mix_total / weight_total[..., None])
        .astype(jnp.bfloat16)
        .reshape(resident_slots, heads_here * HEAD_SIZE)
    )
    row_ids = all_rows
    owner_req = jnp.sum((row_ends[None, :] <= row_ids[:, None]).astype(jnp.int32), axis=1)
    slot_ids = lookup(home_slot, owner_req) * MOST_TREE_NODES + row_ids - lookup(starts, owner_req)
    all_slots = jnp.arange(
        resident_slots * lax.axis_size("req"), dtype=jnp.int32
    )
    pick_slots = (slot_ids[:, None] == all_slots[None, :]).astype(jnp.bfloat16)
    return output(attention, pick_slots, w_out)


def solution(mesh):
    placed = (
        P("tensor", "req"),
        P("req", "tensor"),
        P("req", "tensor"),
        P("tensor", "req"),
        P("req", "tensor", None),
        P("req", None),
        P(),
        P(),
        P(),
    )
    return jax.shard_map(
        body, mesh=mesh, in_specs=placed, out_specs=P("tensor", "req"), check_vma=False
    )
```

```python
import functools
import math

import jax
import jax.numpy as jnp
from jax import lax
from jax.experimental import pallas as pl
from jax.experimental.pallas import tpu as pltpu
from jax.sharding import PartitionSpec as P

HEAD_SIZE = 128
QUERY_HEADS = 64
KEYVALUE_HEADS = 4
MOST_TREE_NODES = 48
CACHE_POSITIONS = 4096
CBLK = 16


ROPE_BASE = 500000.0
NEGATIVE = -1e30


def lookup(table_vals, index_vals):
    table_ids = jnp.arange(table_vals.shape[0], dtype=jnp.int32)
    return jnp.sum(
        jnp.where(index_vals[:, None] == table_ids[None, :], table_vals[None, :], 0), axis=1
    )


def ancestors(parents):
    node_ids = jnp.arange(MOST_TREE_NODES, dtype=jnp.int32)
    linked = (parents[..., :, None] == node_ids).astype(jnp.float32)
    identity = (node_ids[:, None] == node_ids[None, :]).astype(jnp.float32)
    closure = jnp.maximum(linked, identity)
    for sweep in range((MOST_TREE_NODES - 1).bit_length()):
        closure = jnp.minimum(jnp.matmul(closure, closure, precision=lax.Precision.HIGHEST), 1.0)
    return closure


def rotary(tree_depth):
    half_ids = jnp.arange(HEAD_SIZE // 2, dtype=jnp.float32)
    inv_freq = 1.0 / ROPE_BASE ** (half_ids * 2.0 / HEAD_SIZE)
    angles = (tree_depth + CACHE_POSITIONS)[..., None] * inv_freq
    angles = jnp.concatenate([angles, angles], axis=-1)
    return (jnp.cos(angles), jnp.sin(angles))


MESH = pl.DeviceIdType.MESH
VMEM_BYTES = 56 * 1024 * 1024


def inner_of(count):
    inner = 1
    while inner * inner * 4 <= count:
        inner *= 2
    return inner


def target(axis, index):
    other = "tensor" if axis == "req" else "req"
    return {axis: index, other: lax.axis_index(other)}


def place(axis, inner):
    count = lax.axis_size(axis)
    me = lax.axis_index(axis)
    outer = count // inner
    major, minor = me // inner, lax.rem(me, inner)

    def at(step_major, step_minor):
        return lax.rem(major + step_major + outer, outer) * inner + lax.rem(
            minor + step_minor + inner, inner
        )

    return outer, at


def greet(axes):
    barrier = pltpu.get_barrier_semaphore()
    greeted = 0
    for axis, inner in axes:
        outer, at = place(axis, inner)
        steps = [(d, 0) for d in range(1, outer)] + [(0, e) for e in range(1, inner)]
        for d, e in steps:
            pl.semaphore_signal(
                barrier, inc=1, device_id=target(axis, at(d, e)), device_id_type=MESH
            )
            greeted += 1
    pl.semaphore_wait(barrier, greeted)


def remote(source, landing, sems, slot, axis, index):
    return pltpu.make_async_remote_copy(
        src_ref=source,
        dst_ref=landing,
        send_sem=sems[0].at[slot],
        recv_sem=sems[1].at[slot],
        device_id=target(axis, index),
        device_id_type=MESH,
    )


class Gather:
    def __init__(self, axis, inner, part, sems, base=0):
        self.axis, self.inner, self.part, self.sems, self.base = axis, inner, part, sems, base
        self.outer, self.at = place(axis, inner)
        self.started = []

    def copy(self, block, d, e, index):
        return remote(block, block, self.sems, self.base + e * self.outer + d, self.axis, index)

    def start(self):
        own = self.part(self.at(0, 0))
        for d in range(1, self.outer):
            self.started.append(self.copy(own, d, 0, self.at(d, 0)))
            self.started[-1].start()
        for e in range(1, self.inner):
            self.started.append(self.copy(own, 0, e, self.at(0, e)))
            self.started[-1].start()

    def forward(self):
        for d in range(1, self.outer):
            landed = self.part(self.at(-d, 0))
            self.copy(landed, d, 0, self.at(d, 0)).wait_recv()
            for e in range(1, self.inner):
                self.started.append(self.copy(landed, d, e, self.at(0, e)))
                self.started[-1].start()

    def finish(self):
        for e in range(1, self.inner):
            for d in range(self.outer):
                self.copy(self.part(self.at(-d, -e)), d, e, self.at(0, e)).wait_recv()

    def drain(self):
        for copy in self.started:
            copy.wait_send()


class SumScatter:
    def __init__(self, axis, inner, part, near, staged, far, sems, base=0):
        self.axis, self.inner, self.part = axis, inner, part
        self.near, self.staged, self.far = near, staged, far
        self.sems, self.base = sems, base
        self.outer, self.at = place(axis, inner)
        self.order = list(range(1, self.outer)) + [0]
        self.started = []

    def near_copy(self, d, e):
        return remote(
            self.part(self.at(d, e)),
            self.near.at[(e - 1) * self.outer + d],
            self.sems,
            self.base + e * self.outer + d,
            self.axis,
            self.at(0, e),
        )

    def far_copy(self, d):
        return remote(
            self.staged.at[d - 1],
            self.far.at[d - 1],
            self.sems,
            self.base + d,
            self.axis,
            self.at(d, 0),
        )

    def start(self, produce):
        for d in self.order:
            for e in range(1, self.inner):
                produce(self.at(d, e))
                self.started.append(self.near_copy(d, e))
                self.started[-1].start()
        for d in self.order:
            produce(self.at(d, 0))

    def forward(self):
        for d in self.order:
            total = self.part(self.at(d, 0))[...].astype(jnp.float32)
            for e in range(1, self.inner):
                self.near_copy(d, e).wait_recv()
                total = total + self.near[(e - 1) * self.outer + d].astype(jnp.float32)
            if d:
                self.staged[d - 1] = total.astype(jnp.bfloat16)
                self.started.append(self.far_copy(d))
                self.started[-1].start()
        self.total = total

    def finish(self):
        total = self.total
        for d in range(1, self.outer):
            self.far_copy(d).wait_recv()
            total = total + self.far[d - 1].astype(jnp.float32)
        return total.astype(jnp.bfloat16)

    def drain(self):
        for copy in self.started:
            copy.wait_send()


def tiles(width):
    step = 256 if width % 256 == 0 else width
    return width // step, step


CHUNK_HEADS = 4
OUT_PARTS = 2


def kernel(
    req_inner,
    core_inner,
    chunks,
    hidden_ref,
    pick_ref,
    unpick_ref,
    cosine_ref,
    sine_ref,
    tree_ref,
    live_ref,
    wq_ref,
    wkv_ref,
    cache_ref,
    wo_ref,
    out_ref,
    rows,
    wq,
    wkv,
    wo,
    cache,
    kv_all,
    slots,
    mixed_rows,
    load_sem,
    row_send,
    row_recv,
    cache_send,
    cache_recv,
    sum_send,
    sum_recv,
    kv_send,
    kv_recv,
    slot_send,
    slot_recv,
    out_send,
    out_recv,
    *buffers,
):
    tensor_count, req_count = lax.axis_size("tensor"), lax.axis_size("req")
    me, slot = lax.axis_index("tensor"), lax.axis_index("req")
    rows_here = hidden_ref.shape[0]
    query_columns = wq.shape[1]
    heads_here = query_columns // HEAD_SIZE
    group_size = QUERY_HEADS // KEYVALUE_HEADS
    pair = 2 * HEAD_SIZE
    positions = cache_ref.shape[0]
    chunk_width = query_columns // chunks
    chunk_heads = chunk_width // HEAD_SIZE
    score_scale = 1.0 / math.sqrt(HEAD_SIZE)
    loads = [
        pltpu.make_async_copy(source, landing, load_sem.at[i])
        for i, (source, landing) in enumerate(((wkv_ref, wkv), (wq_ref, wq), (wo_ref, wo)))
    ]
    for load in loads:
        load.start()
    greet([("tensor", tensor_count), ("req", req_inner)])

    def row_span(index):
        return pl.ds(pl.multiple_of(index * rows_here, rows_here), rows_here)

    def slot_span(index):
        return pl.ds(pl.multiple_of(index * MOST_TREE_NODES, MOST_TREE_NODES), MOST_TREE_NODES)

    rows[row_span(me), :] = hidden_ref[...]
    row_gather = Gather(
        "tensor", core_inner, lambda index: rows.at[row_span(index)], (row_send, row_recv)
    )
    row_gather.start()
    row_gather.forward()
    row_gather.finish()

    def cache_part(owner, reader):
        head = reader * heads_here // group_size
        return (
            cache_ref.at[:, pl.ds(pl.multiple_of(head * pair, pair), pair)],
            cache.at[pl.ds(pl.multiple_of(owner * positions, positions), positions)],
        )

    own_cache = pltpu.make_async_copy(*cache_part(me, me), load_sem.at[3])
    own_cache.start()
    cache_sems = (cache_send, cache_recv)
    cache_copies = []
    for step in range(1, tensor_count):
        reader = lax.rem(me + step, tensor_count)
        copy = remote(*cache_part(me, reader), cache_sems, step, "tensor", reader)
        copy.start()
        cache_copies.append(copy)

    scatters = []
    for c in range(chunks + 1):
        product, blocks, near, staged, far = buffers[5 * c : 5 * c + 5]
        if c == 0:
            loads[0].wait()
            product[...] = jnp.dot(
                rows[...], wkv[...], preferred_element_type=jnp.float32
            ).astype(jnp.bfloat16)
        else:
            if c == 1:
                loads[1].wait()
            product[...] = jnp.dot(
                rows[...],
                wq[:, (c - 1) * chunk_width : c * chunk_width],
                preferred_element_type=jnp.float32,
            ).astype(jnp.bfloat16)

        def produce(index, blocks=blocks, product=product):
            blocks[slot_span(index), :] = jnp.dot(
                pick_ref[slot_span(index), :], product[...], preferred_element_type=jnp.float32
            ).astype(jnp.bfloat16)

        scatter = SumScatter(
            "req",
            req_inner,
            lambda index, blocks=blocks: blocks.at[slot_span(index)],
            near,
            staged,
            far,
            (sum_send, sum_recv),
            c * req_count,
        )
        scatter.start(produce)
        scatters.append(scatter)

    scatters[0].forward()
    scatters[1].forward()
    kv_all[me] = scatters[0].finish()
    kv_gather = Gather(
        "tensor", tensor_count, lambda index: kv_all.at[index], (kv_send, kv_recv)
    )
    kv_gather.start()
    cosine, sine = cosine_ref[...], sine_ref[...]

    def rotated(values):
        widened = values.astype(jnp.float32)
        turned = jnp.concatenate(
            [widened[:, HEAD_SIZE // 2 :], widened[:, : HEAD_SIZE // 2]], axis=1
        )
        return (widened * cosine + turned * sine).astype(jnp.bfloat16)

    kv_gather.finish()
    kv_head = me * heads_here // group_size
    kv_columns = kv_all.shape[2]
    source_ids = lax.broadcasted_iota(jnp.int32, (kv_columns, pair), 0)
    wanted_ids = lax.broadcasted_iota(jnp.int32, (kv_columns, pair), 1) * KEYVALUE_HEADS + kv_head
    head_kv = jnp.zeros((MOST_TREE_NODES, pair), jnp.float32)
    for t in range(tensor_count):
        chosen = jnp.where(source_ids + t * kv_columns == wanted_ids, 1.0, 0.0)
        head_kv = head_kv + jnp.dot(
            kv_all[t], chosen.astype(jnp.bfloat16), preferred_element_type=jnp.float32
        )
    tree_key = rotated(head_kv[:, :HEAD_SIZE])
    tree_value = head_kv[:, HEAD_SIZE:].astype(jnp.bfloat16)
    own_cache.wait()
    for step in range(1, tensor_count):
        owner = lax.rem(me - step + tensor_count, tensor_count)
        remote(*cache_part(owner, me), cache_sems, step, "tensor", owner).wait_recv()

    def scored(query, key):
        return (
            lax.dot_general(
                query, key, (((1,), (1,)), ((), ())), preferred_element_type=jnp.float32
            )
            * score_scale
        )

    tile = 1024
    gathers = []
    for c in range(chunks):
        if c + 1 < chunks:
            scatters[c + 2].forward()
        found = scatters[c + 1].finish()
        query = jnp.concatenate(
            [rotated(found[:, h * HEAD_SIZE : (h + 1) * HEAD_SIZE]) for h in range(chunk_heads)],
            axis=0,
        )
        scores = scored(query, tree_key) + tree_ref[...]
        top = jnp.max(scores, axis=1, keepdims=True)
        weights = jnp.exp(scores - top)
        total = jnp.sum(weights, axis=1, keepdims=True)
        mix = jnp.dot(
            weights.astype(jnp.bfloat16), tree_value, preferred_element_type=jnp.float32
        )

        def step_tile(i, carry, query=query):
            top, total, mix = carry
            span = pl.ds(pl.multiple_of(i * tile, tile), tile)
            scores = scored(query, cache[span, :HEAD_SIZE]) + live_ref[:, span]
            higher = jnp.maximum(top, jnp.max(scores, axis=1, keepdims=True))
            scale = jnp.exp(top - higher)
            weights = jnp.exp(scores - higher)
            total = total * scale + jnp.sum(weights, axis=1, keepdims=True)
            mix = mix * scale + jnp.dot(
                weights.astype(jnp.bfloat16),
                cache[span, HEAD_SIZE:],
                preferred_element_type=jnp.float32,
            )
            return higher, total, mix

        top, total, mix = lax.fori_loop(
            0, cache.shape[0] // tile, step_tile, (top, total, mix)
        )
        mix = (mix / total).astype(jnp.bfloat16)
        for h in range(chunk_heads):
            low = c * chunk_width + h * HEAD_SIZE
            slots[slot_span(slot), low : low + HEAD_SIZE] = mix[
                h * MOST_TREE_NODES : (h + 1) * MOST_TREE_NODES
            ]
        gather = Gather(
            "req",
            req_inner,
            lambda index, c=c: slots.at[
                slot_span(index), c * chunk_width : (c + 1) * chunk_width
            ],
            (slot_send, slot_recv),
            c * req_count,
        )
        gather.start()
        if gathers:
            gathers[-1].forward()
        gathers.append(gather)
    gathers[-1].forward()
    for c, gather in enumerate(gathers):
        gather.finish()
        columns = slice(c * chunk_width, (c + 1) * chunk_width)
        mixed_rows[:, columns] = jnp.dot(
            unpick_ref[...], slots[:, columns], preferred_element_type=jnp.float32
        ).astype(jnp.bfloat16)

    loads[2].wait()
    out_width = wo.shape[1] // OUT_PARTS
    out_sums = []
    for p in range(OUT_PARTS):
        product, near, staged, far = buffers[5 * (chunks + 1) + 4 * p :][:4]
        steps, step_width = tiles(out_width)

        @pl.loop(0, steps)
        def _(step, p=p, product=product):
            columns = pl.ds(pl.multiple_of(step * step_width, step_width), step_width)
            wide = pl.ds(
                pl.multiple_of(p * out_width + step * step_width, step_width), step_width
            )
            product[:, columns] = jnp.dot(
                mixed_rows[...], wo[:, wide], preferred_element_type=jnp.float32
            ).astype(jnp.bfloat16)

        out_sum = SumScatter(
            "tensor",
            core_inner,
            lambda index, product=product: product.at[row_span(index)],
            near,
            staged,
            far,
            (out_send, out_recv),
            p * tensor_count,
        )
        out_sum.start(lambda index: None)
        out_sums.append(out_sum)
    for out_sum in out_sums:
        out_sum.forward()
    for p, out_sum in enumerate(out_sums):
        out_ref[:, p * out_width : (p + 1) * out_width] = out_sum.finish()
    for work in [row_gather, kv_gather] + scatters + gathers + out_sums:
        work.drain()
    for copy in cache_copies:
        copy.wait_send()


def run(hidden, tables, w_query, keyvalue_weight, cache, w_out):
    tensor_count, req_count = lax.axis_size("tensor"), lax.axis_size("req")
    req_inner, core_inner = inner_of(req_count), 2
    rows_here, width = hidden.shape
    row_total = rows_here * tensor_count
    query_columns, kv_columns = w_query.shape[1], keyvalue_weight.shape[1]
    chunks = query_columns // HEAD_SIZE // CHUNK_HEADS
    depth, out_columns = w_out.shape
    bf16, dma = jnp.bfloat16, pltpu.SemaphoreType.DMA
    any_space, vmem = pl.BlockSpec(memory_space=pl.ANY), pl.BlockSpec(memory_space=pltpu.VMEM)
    outer, core_outer = req_count // req_inner, tensor_count // core_inner
    buffers = []
    for columns in [kv_columns] + [query_columns // chunks] * chunks:
        buffers += [
            pltpu.VMEM((row_total, columns), bf16),
            pltpu.VMEM((req_count * MOST_TREE_NODES, columns), bf16),
            pltpu.VMEM(((req_inner - 1) * outer, MOST_TREE_NODES, columns), bf16),
            pltpu.VMEM((outer - 1, MOST_TREE_NODES, columns), bf16),
            pltpu.VMEM((outer - 1, MOST_TREE_NODES, columns), bf16),
        ]
    for part in range(OUT_PARTS):
        columns = out_columns // OUT_PARTS
        buffers += [
            pltpu.VMEM((row_total, columns), bf16),
            pltpu.VMEM(((core_inner - 1) * core_outer, rows_here, columns), bf16),
            pltpu.VMEM((core_outer - 1, rows_here, columns), bf16),
            pltpu.VMEM((core_outer - 1, rows_here, columns), bf16),
        ]
    sems = [tensor_count, tensor_count, (chunks + 1) * req_count, tensor_count]
    sems += [chunks * req_count, OUT_PARTS * tensor_count]
    return pl.pallas_call(
        functools.partial(kernel, req_inner, core_inner, chunks),
        out_shape=jax.ShapeDtypeStruct((rows_here, out_columns), bf16),
        in_specs=[vmem] * 7 + [any_space] * 4,
        out_specs=vmem,
        scratch_shapes=[
            pltpu.VMEM((row_total, width), bf16),
            pltpu.VMEM(w_query.shape, bf16),
            pltpu.VMEM(keyvalue_weight.shape, bf16),
            pltpu.VMEM(w_out.shape, bf16),
            pltpu.VMEM((cache.shape[0] * tensor_count, 2 * HEAD_SIZE), bf16),
            pltpu.VMEM((tensor_count, MOST_TREE_NODES, kv_columns), bf16),
            pltpu.VMEM((req_count * MOST_TREE_NODES, depth), bf16),
            pltpu.VMEM((row_total, depth), bf16),
            dma((4,)),
        ]
        + [dma((count,)) for count in sems for both in range(2)]
        + buffers,
        compiler_params=pltpu.CompilerParams(
            collective_id=0, has_side_effects=True, vmem_limit_bytes=VMEM_BYTES
        ),
    )(hidden, *tables, w_query, keyvalue_weight, cache, w_out)


def body(
    hidden,
    w_query,
    keyvalue_weight,
    w_out,
    keyvalue_cache,
    cache_live,
    tree_size,
    tree_parent,
    slot_request,
):
    tensor_count = lax.axis_size("tensor")
    req_index = lax.axis_index("req")
    resident_requests = keyvalue_cache.shape[0]
    resident_slots = resident_requests * MOST_TREE_NODES
    row_total = hidden.shape[0] * tensor_count
    row_ends = jnp.cumsum(tree_size)
    starts = row_ends - tree_size
    request_ids = jnp.arange(tree_size.shape[0], dtype=jnp.int32)
    home_slot = jnp.sum(
        jnp.where(slot_request[None, :] == request_ids[:, None], request_ids[None, :], 0), axis=1
    )
    slot_ids = jnp.arange(resident_slots * lax.axis_size("req"), dtype=jnp.int32)
    owner_req = lookup(slot_request, slot_ids // MOST_TREE_NODES)
    node_ids = slot_ids % MOST_TREE_NODES
    is_valid = node_ids < lookup(tree_size, owner_req)
    row_ids = jnp.minimum(lookup(starts, owner_req) + node_ids, row_total - 1)
    all_rows = jnp.arange(row_total, dtype=jnp.int32)
    pick_rows = (
        (row_ids[:, None] == all_rows[None, :]) & is_valid[:, None]
    ).astype(jnp.bfloat16)
    my_requests = lax.dynamic_slice_in_dim(
        slot_request, req_index * resident_requests, resident_requests
    )
    parents = jnp.sum(
        jnp.where(
            my_requests[:, None, None] == request_ids[None, :, None], tree_parent[None, :, :], 0
        ),
        axis=1,
    )
    closure = ancestors(parents)
    tree_depth = jnp.sum(closure, axis=-1) - 1.0
    cosine_table, sine_table = rotary(tree_depth.reshape(resident_slots))
    signed_sine = sine_table * jnp.where(jnp.arange(HEAD_SIZE) < HEAD_SIZE // 2, -1.0, 1.0)
    tree_bias = jnp.tile(jnp.where(closure[0] > 0.5, 0.0, NEGATIVE), (CHUNK_HEADS, 1))
    live_bias = jnp.where(jnp.repeat(cache_live, CBLK, axis=1) > 0, 0.0, NEGATIVE)
    row_ids = all_rows
    owner_req = jnp.sum((row_ends[None, :] <= row_ids[:, None]).astype(jnp.int32), axis=1)
    slot_ids = lookup(home_slot, owner_req) * MOST_TREE_NODES + row_ids - lookup(starts, owner_req)
    all_slots = jnp.arange(
        resident_slots * lax.axis_size("req"), dtype=jnp.int32
    )
    pick_slots = (slot_ids[:, None] == all_slots[None, :]).astype(jnp.bfloat16)
    tables = (pick_rows, pick_slots, cosine_table, signed_sine, tree_bias, live_bias)
    return run(hidden, tables, w_query, keyvalue_weight, keyvalue_cache[0], w_out)


def solution(mesh):
    placed = (
        P("tensor", "req"),
        P("req", "tensor"),
        P("req", "tensor"),
        P("tensor", "req"),
        P("req", "tensor", None),
        P("req", None),
        P(),
        P(),
        P(),
    )
    return jax.shard_map(
        body, mesh=mesh, in_specs=placed, out_specs=P("tensor", "req"), check_vma=False
    )
```

```python
import functools
import math

import jax
import jax.numpy as jnp
import numpy as np
from jax import lax
from jax.experimental import pallas as pl
from jax.experimental.pallas import tpu as pltpu
from jax.sharding import PartitionSpec as P

HEAD_SIZE = 128
QUERY_HEADS = 64
KEYVALUE_HEADS = 4
MOST_TREE_NODES = 48
CACHE_POSITIONS = 4096
CBLK = 16


ROPE_BASE = 500000.0
NEGATIVE = -1e30


def rotary_tables():
    half_ids = np.arange(HEAD_SIZE // 2, dtype=np.float32)
    inv_freq = (1.0 / ROPE_BASE ** (half_ids * 2.0 / HEAD_SIZE)).astype(np.float32)
    positions = np.arange(MOST_TREE_NODES, dtype=np.float32) + CACHE_POSITIONS
    angles = (positions[:, None] * inv_freq).astype(np.float32).astype(np.float64)
    cosine, sine = np.cos(angles), np.sin(angles)
    return np.concatenate([cosine, cosine, -sine, sine], axis=1).astype(np.float32)


MESH = pl.DeviceIdType.MESH
VMEM_BYTES = 56 * 1024 * 1024


def inner_of(count):
    inner = 1
    while inner * inner * 4 <= count:
        inner *= 2
    return inner


def target(axis, index):
    other = "tensor" if axis == "req" else "req"
    return {axis: index, other: lax.axis_index(other)}


def place(axis, inner):
    count = lax.axis_size(axis)
    me = lax.axis_index(axis)
    outer = count // inner
    major, minor = me // inner, lax.rem(me, inner)

    def at(step_major, step_minor):
        return lax.rem(major + step_major + outer, outer) * inner + lax.rem(
            minor + step_minor + inner, inner
        )

    return outer, at


def greet(axes):
    barrier = pltpu.get_barrier_semaphore()
    greeted = 0
    for axis, inner in axes:
        outer, at = place(axis, inner)
        steps = [(d, 0) for d in range(1, outer)] + [(0, e) for e in range(1, inner)]
        for d, e in steps:
            pl.semaphore_signal(
                barrier, inc=1, device_id=target(axis, at(d, e)), device_id_type=MESH
            )
            greeted += 1
    pl.semaphore_wait(barrier, greeted)


def remote(source, landing, sems, slot, axis, index):
    return pltpu.make_async_remote_copy(
        src_ref=source,
        dst_ref=landing,
        send_sem=sems[0].at[slot],
        recv_sem=sems[1].at[slot],
        device_id=target(axis, index),
        device_id_type=MESH,
    )


class Gather:
    def __init__(self, axis, inner, part, sems, base=0):
        self.axis, self.inner, self.part, self.sems, self.base = axis, inner, part, sems, base
        self.outer, self.at = place(axis, inner)
        self.started = []

    def copy(self, block, d, e, index):
        return remote(block, block, self.sems, self.base + e * self.outer + d, self.axis, index)

    def start(self):
        own = self.part(self.at(0, 0))
        for d in range(1, self.outer):
            self.started.append(self.copy(own, d, 0, self.at(d, 0)))
            self.started[-1].start()
        for e in range(1, self.inner):
            self.started.append(self.copy(own, 0, e, self.at(0, e)))
            self.started[-1].start()

    def forward(self):
        for d in range(1, self.outer):
            landed = self.part(self.at(-d, 0))
            self.copy(landed, d, 0, self.at(d, 0)).wait_recv()
            for e in range(1, self.inner):
                self.started.append(self.copy(landed, d, e, self.at(0, e)))
                self.started[-1].start()

    def finish(self):
        for e in range(1, self.inner):
            for d in range(self.outer):
                self.copy(self.part(self.at(-d, -e)), d, e, self.at(0, e)).wait_recv()

    def drain(self):
        for copy in self.started:
            copy.wait_send()


class SumScatter:
    def __init__(self, axis, inner, part, near, staged, far, sems, base=0):
        self.axis, self.inner, self.part = axis, inner, part
        self.near, self.staged, self.far = near, staged, far
        self.sems, self.base = sems, base
        self.outer, self.at = place(axis, inner)
        self.order = list(range(1, self.outer)) + [0]
        self.started = []

    def near_copy(self, d, e):
        return remote(
            self.part(self.at(d, e)),
            self.near.at[(e - 1) * self.outer + d],
            self.sems,
            self.base + e * self.outer + d,
            self.axis,
            self.at(0, e),
        )

    def far_copy(self, d):
        return remote(
            self.staged.at[d - 1],
            self.far.at[d - 1],
            self.sems,
            self.base + d,
            self.axis,
            self.at(d, 0),
        )

    def start(self, produce):
        for d in self.order:
            for e in range(1, self.inner):
                produce(self.at(d, e))
                self.started.append(self.near_copy(d, e))
                self.started[-1].start()
        for d in self.order:
            produce(self.at(d, 0))

    def forward(self):
        for d in self.order:
            total = self.part(self.at(d, 0))[...].astype(jnp.float32)
            for e in range(1, self.inner):
                self.near_copy(d, e).wait_recv()
                total = total + self.near[(e - 1) * self.outer + d].astype(jnp.float32)
            if d:
                self.staged[d - 1] = total.astype(jnp.bfloat16)
                self.started.append(self.far_copy(d))
                self.started[-1].start()
        self.total = total

    def finish(self):
        total = self.total
        for d in range(1, self.outer):
            self.far_copy(d).wait_recv()
            total = total + self.far[d - 1].astype(jnp.float32)
        return total.astype(jnp.bfloat16)

    def drain(self):
        for copy in self.started:
            copy.wait_send()


def tiles(width):
    step = 256 if width % 256 == 0 else width
    return width // step, step


CHUNK_HEADS = 4
OUT_PARTS = 2


def kernel(
    req_inner,
    core_inner,
    chunks,
    hidden_ref,
    rotary_ref,
    block_live_ref,
    parent_ref,
    size_ref,
    owner_ref,
    wq_ref,
    wkv_ref,
    cache_ref,
    wo_ref,
    out_ref,
    rows,
    wq,
    wkv,
    wo,
    cache,
    kv_all,
    slots,
    mixed_rows,
    pick_ref,
    unpick_ref,
    live_ref,
    load_sem,
    row_send,
    row_recv,
    cache_send,
    cache_recv,
    sum_send,
    sum_recv,
    kv_send,
    kv_recv,
    slot_send,
    slot_recv,
    out_send,
    out_recv,
    *buffers,
):
    tensor_count, req_count = lax.axis_size("tensor"), lax.axis_size("req")
    me, slot = lax.axis_index("tensor"), lax.axis_index("req")
    rows_here = hidden_ref.shape[0]
    query_columns = wq.shape[1]
    heads_here = query_columns // HEAD_SIZE
    group_size = QUERY_HEADS // KEYVALUE_HEADS
    pair = 2 * HEAD_SIZE
    positions = cache_ref.shape[0]
    chunk_width = query_columns // chunks
    chunk_heads = chunk_width // HEAD_SIZE
    score_scale = 1.0 / math.sqrt(HEAD_SIZE)
    loads = [
        pltpu.make_async_copy(source, landing, load_sem.at[i])
        for i, (source, landing) in enumerate(((wkv_ref, wkv), (wq_ref, wq), (wo_ref, wo)))
    ]
    for load in loads:
        load.start()
    greet([("tensor", tensor_count), ("req", req_inner)])

    def row_span(index):
        return pl.ds(pl.multiple_of(index * rows_here, rows_here), rows_here)

    def slot_span(index):
        return pl.ds(pl.multiple_of(index * MOST_TREE_NODES, MOST_TREE_NODES), MOST_TREE_NODES)

    rows[row_span(me), :] = hidden_ref[...]
    row_gather = Gather(
        "tensor", core_inner, lambda index: rows.at[row_span(index)], (row_send, row_recv)
    )
    row_gather.start()
    requests = size_ref.shape[0]
    sizes = [size_ref[r] for r in range(requests)]
    owners = [owner_ref[s] for s in range(requests)]
    slot_sizes, slot_starts = [], []
    for owner in owners:
        size, start = jnp.int32(0), jnp.int32(0)
        for r in range(requests):
            size = size + jnp.where(owner == r, sizes[r], 0)
            start = start + jnp.where(owner > r, sizes[r], 0)
        slot_sizes.append(size)
        slot_starts.append(start)
    row_total = rows.shape[0]
    block_shape = (MOST_TREE_NODES, row_total)
    block_nodes = lax.broadcasted_iota(jnp.int32, block_shape, 0)
    block_lag = lax.broadcasted_iota(jnp.int32, block_shape, 1) - block_nodes
    for s in range(requests):
        pick_ref[s * MOST_TREE_NODES : (s + 1) * MOST_TREE_NODES, :] = jnp.where(
            (block_lag == slot_starts[s]) & (block_nodes < slot_sizes[s]), 1.0, 0.0
        ).astype(jnp.bfloat16)
    row_gather.forward()
    row_gather.finish()

    def cache_part(owner, reader):
        head = reader * heads_here // group_size
        return (
            cache_ref.at[:, pl.ds(pl.multiple_of(head * pair, pair), pair)],
            cache.at[pl.ds(pl.multiple_of(owner * positions, positions), positions)],
        )

    own_cache = pltpu.make_async_copy(*cache_part(me, me), load_sem.at[3])
    own_cache.start()
    cache_sems = (cache_send, cache_recv)
    cache_copies = []
    for step in range(1, tensor_count):
        reader = lax.rem(me + step, tensor_count)
        copy = remote(*cache_part(me, reader), cache_sems, step, "tensor", reader)
        copy.start()
        cache_copies.append(copy)

    scatters = []
    for c in range(chunks + 1):
        product, blocks, near, staged, far = buffers[5 * c : 5 * c + 5]
        if c == 0:
            loads[0].wait()
            product[...] = jnp.dot(
                rows[...], wkv[...], preferred_element_type=jnp.float32
            ).astype(jnp.bfloat16)
        else:
            if c == 1:
                loads[1].wait()
            product[...] = jnp.dot(
                rows[...],
                wq[:, (c - 1) * chunk_width : c * chunk_width],
                preferred_element_type=jnp.float32,
            ).astype(jnp.bfloat16)

        def produce(index, blocks=blocks, product=product):
            blocks[slot_span(index), :] = jnp.dot(
                pick_ref[slot_span(index), :], product[...], preferred_element_type=jnp.float32
            ).astype(jnp.bfloat16)

        scatter = SumScatter(
            "req",
            req_inner,
            lambda index, blocks=blocks: blocks.at[slot_span(index)],
            near,
            staged,
            far,
            (sum_send, sum_recv),
            c * req_count,
        )
        scatter.start(produce)
        scatters.append(scatter)

    unpick_shape = unpick_ref.shape
    slot_columns = lax.broadcasted_iota(jnp.int32, (1, unpick_shape[1]), 1)
    lag = jnp.full((1, unpick_shape[1]), -unpick_shape[0] - unpick_shape[1], jnp.int32)
    for s in range(requests):
        nodes = slot_columns - s * MOST_TREE_NODES
        inside = (nodes >= 0) & (nodes < slot_sizes[s])
        lag = jnp.where(inside, slot_starts[s] - s * MOST_TREE_NODES, lag)
    unpick_lag = lax.broadcasted_iota(
        jnp.int32, unpick_shape, 0
    ) - lax.broadcasted_iota(jnp.int32, unpick_shape, 1)
    unpick_ref[...] = jnp.where(unpick_lag == lag, 1.0, 0.0).astype(jnp.bfloat16)

    scatters[0].forward()
    tile = 1024
    block_live = jnp.where(block_live_ref[...] > 0, 1.0, 0.0).astype(jnp.bfloat16)
    block_live = jnp.broadcast_to(block_live, (16, block_live.shape[1]))

    @pl.loop(0, cache.shape[0] // tile)
    def _(i):
        shape = (block_live.shape[1], tile)
        offset = (
            lax.broadcasted_iota(jnp.int32, shape, 1)
            + i * tile
            - lax.broadcasted_iota(jnp.int32, shape, 0) * CBLK
        )
        spread = jnp.where((offset >= 0) & (offset < CBLK), 1.0, 0.0).astype(jnp.bfloat16)
        alive = jnp.dot(block_live, spread, preferred_element_type=jnp.float32)
        live_ref[:, pl.ds(pl.multiple_of(i * tile, tile), tile)] = jnp.where(
            alive[:1] > 0.5, 0.0, NEGATIVE
        )

    square = (MOST_TREE_NODES, MOST_TREE_NODES)
    node_rows = lax.broadcasted_iota(jnp.int32, square, 0)
    node_columns = lax.broadcasted_iota(jnp.int32, square, 1)
    parents = parent_ref[pl.ds(owner_ref[slot], 1), :].astype(jnp.float32)
    parents = jnp.sum(
        jnp.where(node_rows == node_columns, parents, 0.0), axis=1, keepdims=True
    ).astype(jnp.int32)
    closure = jnp.where((node_rows == node_columns) | (node_columns == parents), 1.0, 0.0)
    for sweep in range((MOST_TREE_NODES - 1).bit_length()):
        link = closure.astype(jnp.bfloat16)
        closure = jnp.minimum(jnp.dot(link, link, preferred_element_type=jnp.float32), 1.0)
    depth = jnp.sum(closure, axis=1, keepdims=True).astype(jnp.int32) - 1
    at_depth = jnp.where(node_columns == depth, 1.0, 0.0)
    rotary = jnp.dot(
        at_depth,
        rotary_ref[...],
        preferred_element_type=jnp.float32,
        precision=lax.Precision.HIGHEST,
    )
    cosine, sine = rotary[:, :HEAD_SIZE], rotary[:, HEAD_SIZE:]
    tree_bias = jnp.where(closure > 0.5, 0.0, NEGATIVE)
    tree_bias = jnp.concatenate([tree_bias] * chunk_heads, axis=0)
    scatters[1].forward()
    kv_all[me] = scatters[0].finish()
    kv_gather = Gather(
        "tensor", tensor_count, lambda index: kv_all.at[index], (kv_send, kv_recv)
    )
    kv_gather.start()

    def rotated(values):
        widened = values.astype(jnp.float32)
        turned = jnp.concatenate(
            [widened[:, HEAD_SIZE // 2 :], widened[:, : HEAD_SIZE // 2]], axis=1
        )
        return (widened * cosine + turned * sine).astype(jnp.bfloat16)

    kv_gather.finish()
    kv_head = me * heads_here // group_size
    kv_columns = kv_all.shape[2]
    source_ids = lax.broadcasted_iota(jnp.int32, (kv_columns, pair), 0)
    wanted_ids = lax.broadcasted_iota(jnp.int32, (kv_columns, pair), 1) * KEYVALUE_HEADS + kv_head
    head_kv = jnp.zeros((MOST_TREE_NODES, pair), jnp.float32)
    for t in range(tensor_count):
        chosen = jnp.where(source_ids + t * kv_columns == wanted_ids, 1.0, 0.0)
        head_kv = head_kv + jnp.dot(
            kv_all[t], chosen.astype(jnp.bfloat16), preferred_element_type=jnp.float32
        )
    tree_key = rotated(head_kv[:, :HEAD_SIZE])
    tree_value = head_kv[:, HEAD_SIZE:].astype(jnp.bfloat16)
    own_cache.wait()
    for step in range(1, tensor_count):
        owner = lax.rem(me - step + tensor_count, tensor_count)
        remote(*cache_part(owner, me), cache_sems, step, "tensor", owner).wait_recv()

    def scored(query, key):
        return (
            lax.dot_general(
                query, key, (((1,), (1,)), ((), ())), preferred_element_type=jnp.float32
            )
            * score_scale
        )

    gathers = []
    for c in range(chunks):
        if c + 1 < chunks:
            scatters[c + 2].forward()
        found = scatters[c + 1].finish()
        query = jnp.concatenate(
            [rotated(found[:, h * HEAD_SIZE : (h + 1) * HEAD_SIZE]) for h in range(chunk_heads)],
            axis=0,
        )
        scores = scored(query, tree_key) + tree_bias
        top = jnp.max(scores, axis=1, keepdims=True)
        weights = jnp.exp(scores - top)
        total = jnp.sum(weights, axis=1, keepdims=True)
        mix = jnp.dot(
            weights.astype(jnp.bfloat16), tree_value, preferred_element_type=jnp.float32
        )

        def step_tile(i, carry, query=query):
            top, total, mix = carry
            span = pl.ds(pl.multiple_of(i * tile, tile), tile)
            scores = scored(query, cache[span, :HEAD_SIZE]) + live_ref[:, span]
            higher = jnp.maximum(top, jnp.max(scores, axis=1, keepdims=True))
            scale = jnp.exp(top - higher)
            weights = jnp.exp(scores - higher)
            total = total * scale + jnp.sum(weights, axis=1, keepdims=True)
            mix = mix * scale + jnp.dot(
                weights.astype(jnp.bfloat16),
                cache[span, HEAD_SIZE:],
                preferred_element_type=jnp.float32,
            )
            return higher, total, mix

        top, total, mix = lax.fori_loop(
            0, cache.shape[0] // tile, step_tile, (top, total, mix)
        )
        mix = (mix / total).astype(jnp.bfloat16)
        for h in range(chunk_heads):
            low = c * chunk_width + h * HEAD_SIZE
            slots[slot_span(slot), low : low + HEAD_SIZE] = mix[
                h * MOST_TREE_NODES : (h + 1) * MOST_TREE_NODES
            ]
        gather = Gather(
            "req",
            req_inner,
            lambda index, c=c: slots.at[
                slot_span(index), c * chunk_width : (c + 1) * chunk_width
            ],
            (slot_send, slot_recv),
            c * req_count,
        )
        gather.start()
        if gathers:
            gathers[-1].forward()
        gathers.append(gather)
    gathers[-1].forward()
    for c, gather in enumerate(gathers):
        gather.finish()
        columns = slice(c * chunk_width, (c + 1) * chunk_width)
        mixed_rows[:, columns] = jnp.dot(
            unpick_ref[...], slots[:, columns], preferred_element_type=jnp.float32
        ).astype(jnp.bfloat16)

    loads[2].wait()
    out_width = wo.shape[1] // OUT_PARTS
    out_sums = []
    for p in range(OUT_PARTS):
        product, near, staged, far = buffers[5 * (chunks + 1) + 4 * p :][:4]
        steps, step_width = tiles(out_width)

        @pl.loop(0, steps)
        def _(step, p=p, product=product):
            columns = pl.ds(pl.multiple_of(step * step_width, step_width), step_width)
            wide = pl.ds(
                pl.multiple_of(p * out_width + step * step_width, step_width), step_width
            )
            product[:, columns] = jnp.dot(
                mixed_rows[...], wo[:, wide], preferred_element_type=jnp.float32
            ).astype(jnp.bfloat16)

        out_sum = SumScatter(
            "tensor",
            core_inner,
            lambda index, product=product: product.at[row_span(index)],
            near,
            staged,
            far,
            (out_send, out_recv),
            p * tensor_count,
        )
        out_sum.start(lambda index: None)
        out_sums.append(out_sum)
    for out_sum in out_sums:
        out_sum.forward()
    for p, out_sum in enumerate(out_sums):
        out_ref[:, p * out_width : (p + 1) * out_width] = out_sum.finish()
    for work in [row_gather, kv_gather] + scatters + gathers + out_sums:
        work.drain()
    for copy in cache_copies:
        copy.wait_send()


def run(hidden, tables, w_query, keyvalue_weight, cache, w_out):
    tensor_count, req_count = lax.axis_size("tensor"), lax.axis_size("req")
    req_inner, core_inner = inner_of(req_count), 2
    rows_here, width = hidden.shape
    row_total = rows_here * tensor_count
    query_columns, kv_columns = w_query.shape[1], keyvalue_weight.shape[1]
    chunks = query_columns // HEAD_SIZE // CHUNK_HEADS
    depth, out_columns = w_out.shape
    bf16, dma = jnp.bfloat16, pltpu.SemaphoreType.DMA
    any_space, vmem = pl.BlockSpec(memory_space=pl.ANY), pl.BlockSpec(memory_space=pltpu.VMEM)
    outer, core_outer = req_count // req_inner, tensor_count // core_inner
    buffers = []
    for columns in [kv_columns] + [query_columns // chunks] * chunks:
        buffers += [
            pltpu.VMEM((row_total, columns), bf16),
            pltpu.VMEM((req_count * MOST_TREE_NODES, columns), bf16),
            pltpu.VMEM(((req_inner - 1) * outer, MOST_TREE_NODES, columns), bf16),
            pltpu.VMEM((outer - 1, MOST_TREE_NODES, columns), bf16),
            pltpu.VMEM((outer - 1, MOST_TREE_NODES, columns), bf16),
        ]
    for part in range(OUT_PARTS):
        columns = out_columns // OUT_PARTS
        buffers += [
            pltpu.VMEM((row_total, columns), bf16),
            pltpu.VMEM(((core_inner - 1) * core_outer, rows_here, columns), bf16),
            pltpu.VMEM((core_outer - 1, rows_here, columns), bf16),
            pltpu.VMEM((core_outer - 1, rows_here, columns), bf16),
        ]
    sems = [tensor_count, tensor_count, (chunks + 1) * req_count, tensor_count]
    sems += [chunks * req_count, OUT_PARTS * tensor_count]
    return pl.pallas_call(
        functools.partial(kernel, req_inner, core_inner, chunks),
        out_shape=jax.ShapeDtypeStruct((rows_here, out_columns), bf16),
        in_specs=[vmem] * 4 + [pl.BlockSpec(memory_space=pltpu.SMEM)] * 2 + [any_space] * 4,
        out_specs=vmem,
        scratch_shapes=[
            pltpu.VMEM((row_total, width), bf16),
            pltpu.VMEM(w_query.shape, bf16),
            pltpu.VMEM(keyvalue_weight.shape, bf16),
            pltpu.VMEM(w_out.shape, bf16),
            pltpu.VMEM((cache.shape[0] * tensor_count, 2 * HEAD_SIZE), bf16),
            pltpu.VMEM((tensor_count, MOST_TREE_NODES, kv_columns), bf16),
            pltpu.VMEM((req_count * MOST_TREE_NODES, depth), bf16),
            pltpu.VMEM((row_total, depth), bf16),
            pltpu.VMEM((req_count * MOST_TREE_NODES, row_total), bf16),
            pltpu.VMEM((row_total, req_count * MOST_TREE_NODES), bf16),
            pltpu.VMEM((1, CACHE_POSITIONS), jnp.float32),
            dma((4,)),
        ]
        + [dma((count,)) for count in sems for both in range(2)]
        + buffers,
        compiler_params=pltpu.CompilerParams(
            collective_id=0, has_side_effects=True, vmem_limit_bytes=VMEM_BYTES
        ),
    )(hidden, *tables, w_query, keyvalue_weight, cache, w_out)


def body(
    hidden,
    w_query,
    keyvalue_weight,
    w_out,
    keyvalue_cache,
    cache_live,
    tree_size,
    tree_parent,
    slot_request,
):
    tables = (rotary_tables(), cache_live, tree_parent, tree_size, slot_request)
    return run(hidden, tables, w_query, keyvalue_weight, keyvalue_cache[0], w_out)


def solution(mesh):
    placed = (
        P("tensor", "req"),
        P("req", "tensor"),
        P("req", "tensor"),
        P("tensor", "req"),
        P("req", "tensor", None),
        P("req", None),
        P(),
        P(),
        P(),
    )
    return jax.shard_map(
        body, mesh=mesh, in_specs=placed, out_specs=P("tensor", "req"), check_vma=False
    )
```

```python
import functools
import math

import jax
import jax.numpy as jnp
import numpy as np
from jax import lax
from jax.experimental import pallas as pl
from jax.experimental.pallas import tpu as pltpu
from jax.sharding import PartitionSpec as P

HEAD_SIZE = 128
QUERY_HEADS = 64
KEYVALUE_HEADS = 4
MOST_TREE_NODES = 48
CACHE_POSITIONS = 4096
CBLK = 16


ROPE_BASE = 500000.0
NEGATIVE = -1e30


def rotary_tables():
    half_ids = np.arange(HEAD_SIZE // 2, dtype=np.float32)
    inv_freq = (1.0 / ROPE_BASE ** (half_ids * 2.0 / HEAD_SIZE)).astype(np.float32)
    positions = np.arange(MOST_TREE_NODES, dtype=np.float32) + CACHE_POSITIONS
    angles = (positions[:, None] * inv_freq).astype(np.float32).astype(np.float64)
    cosine, sine = np.cos(angles), np.sin(angles)
    return np.concatenate([cosine, cosine, -sine, sine], axis=1).astype(np.float32)


MESH = pl.DeviceIdType.MESH
VMEM_BYTES = 56 * 1024 * 1024


def inner_of(count):
    inner = 1
    while inner * inner * 4 <= count:
        inner *= 2
    return inner


def target(axis, index):
    other = "tensor" if axis == "req" else "req"
    return {axis: index, other: lax.axis_index(other)}


def place(axis, inner):
    count = lax.axis_size(axis)
    me = lax.axis_index(axis)
    outer = count // inner
    major, minor = me // inner, lax.rem(me, inner)

    def at(step_major, step_minor):
        return lax.rem(major + step_major + outer, outer) * inner + lax.rem(
            minor + step_minor + inner, inner
        )

    return outer, at


def greet(axes):
    barrier = pltpu.get_barrier_semaphore()
    greeted = 0
    for axis, inner in axes:
        outer, at = place(axis, inner)
        steps = [(d, 0) for d in range(1, outer)] + [(0, e) for e in range(1, inner)]
        for d, e in steps:
            pl.semaphore_signal(
                barrier, inc=1, device_id=target(axis, at(d, e)), device_id_type=MESH
            )
            greeted += 1
    pl.semaphore_wait(barrier, greeted)


def remote(source, landing, sems, slot, axis, index):
    return pltpu.make_async_remote_copy(
        src_ref=source,
        dst_ref=landing,
        send_sem=sems[0].at[slot],
        recv_sem=sems[1].at[slot],
        device_id=target(axis, index),
        device_id_type=MESH,
    )


class Gather:
    def __init__(self, axis, inner, part, sems, base=0):
        self.axis, self.inner, self.part, self.sems, self.base = axis, inner, part, sems, base
        self.outer, self.at = place(axis, inner)
        self.started = []

    def copy(self, block, d, e, index):
        return remote(block, block, self.sems, self.base + e * self.outer + d, self.axis, index)

    def start(self):
        own = self.part(self.at(0, 0))
        for d in range(1, self.outer):
            self.started.append(self.copy(own, d, 0, self.at(d, 0)))
            self.started[-1].start()
        for e in range(1, self.inner):
            self.started.append(self.copy(own, 0, e, self.at(0, e)))
            self.started[-1].start()

    def forward(self):
        for d in range(1, self.outer):
            landed = self.part(self.at(-d, 0))
            self.copy(landed, d, 0, self.at(d, 0)).wait_recv()
            for e in range(1, self.inner):
                self.started.append(self.copy(landed, d, e, self.at(0, e)))
                self.started[-1].start()

    def finish(self):
        for e in range(1, self.inner):
            for d in range(self.outer):
                self.copy(self.part(self.at(-d, -e)), d, e, self.at(0, e)).wait_recv()

    def drain(self):
        for copy in self.started:
            copy.wait_send()


class SumScatter:
    def __init__(self, axis, inner, part, near, staged, far, sems, base=0):
        self.axis, self.inner, self.part = axis, inner, part
        self.near, self.staged, self.far = near, staged, far
        self.sems, self.base = sems, base
        self.outer, self.at = place(axis, inner)
        self.order = list(range(1, self.outer)) + [0]
        self.started = []

    def near_copy(self, d, e):
        return remote(
            self.part(self.at(d, e)),
            self.near.at[(e - 1) * self.outer + d],
            self.sems,
            self.base + e * self.outer + d,
            self.axis,
            self.at(0, e),
        )

    def far_copy(self, d):
        return remote(
            self.staged.at[d - 1],
            self.far.at[d - 1],
            self.sems,
            self.base + d,
            self.axis,
            self.at(d, 0),
        )

    def start(self, produce):
        for d in self.order:
            for e in range(1, self.inner):
                produce(self.at(d, e))
                self.started.append(self.near_copy(d, e))
                self.started[-1].start()
        for d in self.order:
            produce(self.at(d, 0))

    def forward(self):
        for d in self.order:
            total = self.part(self.at(d, 0))[...].astype(jnp.float32)
            for e in range(1, self.inner):
                self.near_copy(d, e).wait_recv()
                total = total + self.near[(e - 1) * self.outer + d].astype(jnp.float32)
            if d:
                self.staged[d - 1] = total.astype(jnp.bfloat16)
                self.started.append(self.far_copy(d))
                self.started[-1].start()
        self.total = total

    def finish(self):
        total = self.total
        for d in range(1, self.outer):
            self.far_copy(d).wait_recv()
            total = total + self.far[d - 1].astype(jnp.float32)
        return total.astype(jnp.bfloat16)

    def drain(self):
        for copy in self.started:
            copy.wait_send()


def tiles(width):
    step = 256 if width % 256 == 0 else width
    return width // step, step


CHUNK_HEADS = 4
OUT_PARTS = 2


def kernel(
    req_inner,
    core_inner,
    chunks,
    hidden_ref,
    rotary_ref,
    block_live_ref,
    parent_ref,
    size_ref,
    owner_ref,
    wq_ref,
    wkv_ref,
    cache_ref,
    wo_ref,
    out_ref,
    rows,
    wq,
    wkv,
    wo,
    cache,
    kv_all,
    slots,
    mixed_rows,
    pick_ref,
    unpick_ref,
    live_ref,
    load_sem,
    row_send,
    row_recv,
    cache_send,
    cache_recv,
    sum_send,
    sum_recv,
    kv_send,
    kv_recv,
    slot_send,
    slot_recv,
    out_send,
    out_recv,
    *buffers,
):
    tensor_count, req_count = lax.axis_size("tensor"), lax.axis_size("req")
    me, slot = lax.axis_index("tensor"), lax.axis_index("req")
    rows_here = hidden_ref.shape[0]
    query_columns = wq.shape[1]
    heads_here = query_columns // HEAD_SIZE
    group_size = QUERY_HEADS // KEYVALUE_HEADS
    pair = 2 * HEAD_SIZE
    positions = cache_ref.shape[0]
    chunk_width = query_columns // chunks
    chunk_heads = chunk_width // HEAD_SIZE
    score_scale = 1.0 / math.sqrt(HEAD_SIZE)
    loads = [
        pltpu.make_async_copy(source, landing, load_sem.at[i])
        for i, (source, landing) in enumerate(((wkv_ref, wkv), (wq_ref, wq), (wo_ref, wo)))
    ]
    for load in loads:
        load.start()
    greet([("tensor", tensor_count), ("req", req_inner)])

    def row_span(index):
        return pl.ds(pl.multiple_of(index * rows_here, rows_here), rows_here)

    def slot_span(index):
        return pl.ds(pl.multiple_of(index * MOST_TREE_NODES, MOST_TREE_NODES), MOST_TREE_NODES)

    rows[row_span(me), :] = hidden_ref[...]
    row_gather = Gather(
        "tensor", core_inner, lambda index: rows.at[row_span(index)], (row_send, row_recv)
    )
    row_gather.start()

    def cache_part(owner, reader):
        head = reader * heads_here // group_size
        return (
            cache_ref.at[:, pl.ds(pl.multiple_of(head * pair, pair), pair)],
            cache.at[pl.ds(pl.multiple_of(owner * positions, positions), positions)],
        )

    own_cache = pltpu.make_async_copy(*cache_part(me, me), load_sem.at[3])
    own_cache.start()
    cache_sems = (cache_send, cache_recv)
    cache_copies = []
    for step in range(1, tensor_count):
        reader = lax.rem(me + step, tensor_count)
        copy = remote(*cache_part(me, reader), cache_sems, step, "tensor", reader)
        copy.start()
        cache_copies.append(copy)

    requests = size_ref.shape[0]
    sizes = [size_ref[r] for r in range(requests)]
    owners = [owner_ref[s] for s in range(requests)]
    slot_sizes, slot_starts = [], []
    for owner in owners:
        size, start = jnp.int32(0), jnp.int32(0)
        for r in range(requests):
            size = size + jnp.where(owner == r, sizes[r], 0)
            start = start + jnp.where(owner > r, sizes[r], 0)
        slot_sizes.append(size)
        slot_starts.append(start)
    row_total = rows.shape[0]
    block_shape = (MOST_TREE_NODES, row_total)
    block_nodes = lax.broadcasted_iota(jnp.int32, block_shape, 0)
    block_lag = lax.broadcasted_iota(jnp.int32, block_shape, 1) - block_nodes
    for s in range(requests):
        pick_ref[s * MOST_TREE_NODES : (s + 1) * MOST_TREE_NODES, :] = jnp.where(
            (block_lag == slot_starts[s]) & (block_nodes < slot_sizes[s]), 1.0, 0.0
        ).astype(jnp.bfloat16)
    row_gather.forward()
    row_gather.finish()

    scatters = []
    for c in range(chunks + 1):
        product, blocks, near, staged, far = buffers[5 * c : 5 * c + 5]
        if c == 0:
            loads[0].wait()
            product[...] = jnp.dot(
                rows[...], wkv[...], preferred_element_type=jnp.float32
            ).astype(jnp.bfloat16)
        else:
            if c == 1:
                loads[1].wait()
            product[...] = jnp.dot(
                rows[...],
                wq[:, (c - 1) * chunk_width : c * chunk_width],
                preferred_element_type=jnp.float32,
            ).astype(jnp.bfloat16)

        def produce(index, blocks=blocks, product=product):
            blocks[slot_span(index), :] = jnp.dot(
                pick_ref[slot_span(index), :], product[...], preferred_element_type=jnp.float32
            ).astype(jnp.bfloat16)

        scatter = SumScatter(
            "req",
            req_inner,
            lambda index, blocks=blocks: blocks.at[slot_span(index)],
            near,
            staged,
            far,
            (sum_send, sum_recv),
            c * req_count,
        )
        scatter.start(produce)
        scatters.append(scatter)

    unpick_shape = unpick_ref.shape
    slot_columns = lax.broadcasted_iota(jnp.int32, (1, unpick_shape[1]), 1)
    lag = jnp.full((1, unpick_shape[1]), -unpick_shape[0] - unpick_shape[1], jnp.int32)
    for s in range(requests):
        nodes = slot_columns - s * MOST_TREE_NODES
        inside = (nodes >= 0) & (nodes < slot_sizes[s])
        lag = jnp.where(inside, slot_starts[s] - s * MOST_TREE_NODES, lag)
    unpick_lag = lax.broadcasted_iota(
        jnp.int32, unpick_shape, 0
    ) - lax.broadcasted_iota(jnp.int32, unpick_shape, 1)
    unpick_ref[...] = jnp.where(unpick_lag == lag, 1.0, 0.0).astype(jnp.bfloat16)

    scatters[0].forward()
    tile = 1024
    block_live = jnp.where(block_live_ref[...] > 0, 1.0, 0.0).astype(jnp.bfloat16)
    block_live = jnp.broadcast_to(block_live, (16, block_live.shape[1]))

    @pl.loop(0, cache.shape[0] // tile)
    def _(i):
        shape = (block_live.shape[1], tile)
        offset = (
            lax.broadcasted_iota(jnp.int32, shape, 1)
            + i * tile
            - lax.broadcasted_iota(jnp.int32, shape, 0) * CBLK
        )
        spread = jnp.where((offset >= 0) & (offset < CBLK), 1.0, 0.0).astype(jnp.bfloat16)
        alive = jnp.dot(block_live, spread, preferred_element_type=jnp.float32)
        live_ref[:, pl.ds(pl.multiple_of(i * tile, tile), tile)] = jnp.where(
            alive[:1] > 0.5, 0.0, NEGATIVE
        )

    square = (MOST_TREE_NODES, MOST_TREE_NODES)
    node_rows = lax.broadcasted_iota(jnp.int32, square, 0)
    node_columns = lax.broadcasted_iota(jnp.int32, square, 1)
    parents = parent_ref[pl.ds(owner_ref[slot], 1), :].astype(jnp.float32)
    parents = jnp.sum(
        jnp.where(node_rows == node_columns, parents, 0.0), axis=1, keepdims=True
    ).astype(jnp.int32)
    closure = jnp.where((node_rows == node_columns) | (node_columns == parents), 1.0, 0.0)
    for sweep in range((MOST_TREE_NODES - 1).bit_length()):
        link = closure.astype(jnp.bfloat16)
        closure = jnp.minimum(jnp.dot(link, link, preferred_element_type=jnp.float32), 1.0)
    depth = jnp.sum(closure, axis=1, keepdims=True).astype(jnp.int32) - 1
    at_depth = jnp.where(node_columns == depth, 1.0, 0.0)
    rotary = jnp.dot(
        at_depth,
        rotary_ref[...],
        preferred_element_type=jnp.float32,
        precision=lax.Precision.HIGHEST,
    )
    cosine, sine = rotary[:, :HEAD_SIZE], rotary[:, HEAD_SIZE:]
    tree_bias = jnp.where(closure > 0.5, 0.0, NEGATIVE)
    tree_bias = jnp.concatenate([tree_bias] * chunk_heads, axis=0)
    scatters[1].forward()
    kv_all[me] = scatters[0].finish()
    kv_gather = Gather(
        "tensor", tensor_count, lambda index: kv_all.at[index], (kv_send, kv_recv)
    )
    kv_gather.start()

    def rotated(values):
        widened = values.astype(jnp.float32)
        turned = jnp.concatenate(
            [widened[:, HEAD_SIZE // 2 :], widened[:, : HEAD_SIZE // 2]], axis=1
        )
        return (widened * cosine + turned * sine).astype(jnp.bfloat16)

    for c in range(2, min(chunks, 3) + 1):
        scatters[c].forward()
    kv_gather.finish()
    kv_head = me * heads_here // group_size
    kv_columns = kv_all.shape[2]
    source_ids = lax.broadcasted_iota(jnp.int32, (kv_columns, pair), 0)
    wanted_ids = lax.broadcasted_iota(jnp.int32, (kv_columns, pair), 1) * KEYVALUE_HEADS + kv_head
    head_kv = jnp.zeros((MOST_TREE_NODES, pair), jnp.float32)
    for t in range(tensor_count):
        chosen = jnp.where(source_ids + t * kv_columns == wanted_ids, 1.0, 0.0)
        head_kv = head_kv + jnp.dot(
            kv_all[t], chosen.astype(jnp.bfloat16), preferred_element_type=jnp.float32
        )
    tree_key = rotated(head_kv[:, :HEAD_SIZE])
    tree_value = head_kv[:, HEAD_SIZE:].astype(jnp.bfloat16)
    own_cache.wait()
    for step in range(1, tensor_count):
        owner = lax.rem(me - step + tensor_count, tensor_count)
        remote(*cache_part(owner, me), cache_sems, step, "tensor", owner).wait_recv()

    def scored(query, key):
        return (
            lax.dot_general(
                query, key, (((1,), (1,)), ((), ())), preferred_element_type=jnp.float32
            )
            * score_scale
        )

    gathers = []
    for c in range(chunks):
        if c + 3 < chunks:
            scatters[c + 4].forward()
        found = scatters[c + 1].finish()
        query = jnp.concatenate(
            [rotated(found[:, h * HEAD_SIZE : (h + 1) * HEAD_SIZE]) for h in range(chunk_heads)],
            axis=0,
        )
        scores = scored(query, tree_key) + tree_bias
        top = jnp.max(scores, axis=1, keepdims=True)
        weights = jnp.exp(scores - top)
        total = jnp.sum(weights, axis=1, keepdims=True)
        mix = jnp.dot(
            weights.astype(jnp.bfloat16), tree_value, preferred_element_type=jnp.float32
        )

        def step_tile(i, carry, query=query):
            top, total, mix = carry
            span = pl.ds(pl.multiple_of(i * tile, tile), tile)
            scores = scored(query, cache[span, :HEAD_SIZE]) + live_ref[:, span]
            higher = jnp.maximum(top, jnp.max(scores, axis=1, keepdims=True))
            scale = jnp.exp(top - higher)
            weights = jnp.exp(scores - higher)
            total = total * scale + jnp.sum(weights, axis=1, keepdims=True)
            mix = mix * scale + jnp.dot(
                weights.astype(jnp.bfloat16),
                cache[span, HEAD_SIZE:],
                preferred_element_type=jnp.float32,
            )
            return higher, total, mix

        top, total, mix = lax.fori_loop(
            0, cache.shape[0] // tile, step_tile, (top, total, mix)
        )
        mix = (mix / total).astype(jnp.bfloat16)
        for h in range(chunk_heads):
            low = c * chunk_width + h * HEAD_SIZE
            slots[slot_span(slot), low : low + HEAD_SIZE] = mix[
                h * MOST_TREE_NODES : (h + 1) * MOST_TREE_NODES
            ]
        gather = Gather(
            "req",
            req_inner,
            lambda index, c=c: slots.at[
                slot_span(index), c * chunk_width : (c + 1) * chunk_width
            ],
            (slot_send, slot_recv),
            c * req_count,
        )
        gather.start()
        if gathers:
            gathers[-1].forward()
        gathers.append(gather)
    gathers[-1].forward()
    for c, gather in enumerate(gathers):
        gather.finish()
        columns = slice(c * chunk_width, (c + 1) * chunk_width)
        mixed_rows[:, columns] = jnp.dot(
            unpick_ref[...], slots[:, columns], preferred_element_type=jnp.float32
        ).astype(jnp.bfloat16)

    loads[2].wait()
    out_width = wo.shape[1] // OUT_PARTS
    out_sums = []
    for p in range(OUT_PARTS):
        product, near, staged, far = buffers[5 * (chunks + 1) + 4 * p :][:4]
        steps, step_width = tiles(out_width)

        @pl.loop(0, steps)
        def _(step, p=p, product=product):
            columns = pl.ds(pl.multiple_of(step * step_width, step_width), step_width)
            wide = pl.ds(
                pl.multiple_of(p * out_width + step * step_width, step_width), step_width
            )
            product[:, columns] = jnp.dot(
                mixed_rows[...], wo[:, wide], preferred_element_type=jnp.float32
            ).astype(jnp.bfloat16)

        out_sum = SumScatter(
            "tensor",
            core_inner,
            lambda index, product=product: product.at[row_span(index)],
            near,
            staged,
            far,
            (out_send, out_recv),
            p * tensor_count,
        )
        out_sum.start(lambda index: None)
        out_sums.append(out_sum)
    for out_sum in out_sums:
        out_sum.forward()
    for p, out_sum in enumerate(out_sums):
        out_ref[:, p * out_width : (p + 1) * out_width] = out_sum.finish()
    for work in [row_gather, kv_gather] + scatters + gathers + out_sums:
        work.drain()
    for copy in cache_copies:
        copy.wait_send()


def run(hidden, tables, w_query, keyvalue_weight, cache, w_out):
    tensor_count, req_count = lax.axis_size("tensor"), lax.axis_size("req")
    req_inner, core_inner = inner_of(req_count), 2
    rows_here, width = hidden.shape
    row_total = rows_here * tensor_count
    query_columns, kv_columns = w_query.shape[1], keyvalue_weight.shape[1]
    chunks = query_columns // HEAD_SIZE // CHUNK_HEADS
    depth, out_columns = w_out.shape
    bf16, dma = jnp.bfloat16, pltpu.SemaphoreType.DMA
    any_space, vmem = pl.BlockSpec(memory_space=pl.ANY), pl.BlockSpec(memory_space=pltpu.VMEM)
    outer, core_outer = req_count // req_inner, tensor_count // core_inner
    buffers = []
    for columns in [kv_columns] + [query_columns // chunks] * chunks:
        buffers += [
            pltpu.VMEM((row_total, columns), bf16),
            pltpu.VMEM((req_count * MOST_TREE_NODES, columns), bf16),
            pltpu.VMEM(((req_inner - 1) * outer, MOST_TREE_NODES, columns), bf16),
            pltpu.VMEM((outer - 1, MOST_TREE_NODES, columns), bf16),
            pltpu.VMEM((outer - 1, MOST_TREE_NODES, columns), bf16),
        ]
    for part in range(OUT_PARTS):
        columns = out_columns // OUT_PARTS
        buffers += [
            pltpu.VMEM((row_total, columns), bf16),
            pltpu.VMEM(((core_inner - 1) * core_outer, rows_here, columns), bf16),
            pltpu.VMEM((core_outer - 1, rows_here, columns), bf16),
            pltpu.VMEM((core_outer - 1, rows_here, columns), bf16),
        ]
    sems = [tensor_count, tensor_count, (chunks + 1) * req_count, tensor_count]
    sems += [chunks * req_count, OUT_PARTS * tensor_count]
    return pl.pallas_call(
        functools.partial(kernel, req_inner, core_inner, chunks),
        out_shape=jax.ShapeDtypeStruct((rows_here, out_columns), bf16),
        in_specs=[vmem] * 4 + [pl.BlockSpec(memory_space=pltpu.SMEM)] * 2 + [any_space] * 4,
        out_specs=vmem,
        scratch_shapes=[
            pltpu.VMEM((row_total, width), bf16),
            pltpu.VMEM(w_query.shape, bf16),
            pltpu.VMEM(keyvalue_weight.shape, bf16),
            pltpu.VMEM(w_out.shape, bf16),
            pltpu.VMEM((cache.shape[0] * tensor_count, 2 * HEAD_SIZE), bf16),
            pltpu.VMEM((tensor_count, MOST_TREE_NODES, kv_columns), bf16),
            pltpu.VMEM((req_count * MOST_TREE_NODES, depth), bf16),
            pltpu.VMEM((row_total, depth), bf16),
            pltpu.VMEM((req_count * MOST_TREE_NODES, row_total), bf16),
            pltpu.VMEM((row_total, req_count * MOST_TREE_NODES), bf16),
            pltpu.VMEM((1, CACHE_POSITIONS), jnp.float32),
            dma((4,)),
        ]
        + [dma((count,)) for count in sems for both in range(2)]
        + buffers,
        compiler_params=pltpu.CompilerParams(
            collective_id=0, has_side_effects=True, vmem_limit_bytes=VMEM_BYTES
        ),
    )(hidden, *tables, w_query, keyvalue_weight, cache, w_out)


def body(
    hidden,
    w_query,
    keyvalue_weight,
    w_out,
    keyvalue_cache,
    cache_live,
    tree_size,
    tree_parent,
    slot_request,
):
    tables = (rotary_tables(), cache_live, tree_parent, tree_size, slot_request)
    return run(hidden, tables, w_query, keyvalue_weight, keyvalue_cache[0], w_out)


def solution(mesh):
    placed = (
        P("tensor", "req"),
        P("req", "tensor"),
        P("req", "tensor"),
        P("tensor", "req"),
        P("req", "tensor", None),
        P("req", None),
        P(),
        P(),
        P(),
    )
    return jax.shard_map(
        body, mesh=mesh, in_specs=placed, out_specs=P("tensor", "req"), check_vma=False
    )
```

```python
import functools
import math

import jax
import jax.numpy as jnp
import numpy as np
from jax import lax
from jax.experimental import pallas as pl
from jax.experimental.pallas import tpu as pltpu
from jax.sharding import PartitionSpec as P

HEAD_SIZE = 128
QUERY_HEADS = 64
KEYVALUE_HEADS = 4
MOST_TREE_NODES = 48
CACHE_POSITIONS = 4096
CBLK = 16


ROPE_BASE = 500000.0
NEGATIVE = -1e30


def rotary_tables():
    half_ids = np.arange(HEAD_SIZE // 2, dtype=np.float32)
    inv_freq = (1.0 / ROPE_BASE ** (half_ids * 2.0 / HEAD_SIZE)).astype(np.float32)
    positions = np.arange(MOST_TREE_NODES, dtype=np.float32) + CACHE_POSITIONS
    angles = (positions[:, None] * inv_freq).astype(np.float32).astype(np.float64)
    cosine, sine = np.cos(angles), np.sin(angles)
    return np.concatenate([cosine, cosine, -sine, sine], axis=1).astype(np.float32)


MESH = pl.DeviceIdType.MESH
VMEM_BYTES = 56 * 1024 * 1024


def inner_of(count):
    inner = 1
    while inner * inner * 4 <= count:
        inner *= 2
    return inner


def target(axis, index):
    other = "tensor" if axis == "req" else "req"
    return {axis: index, other: lax.axis_index(other)}


def place(axis, inner):
    count = lax.axis_size(axis)
    me = lax.axis_index(axis)
    outer = count // inner
    major, minor = me // inner, lax.rem(me, inner)

    def at(step_major, step_minor):
        return lax.rem(major + step_major + outer, outer) * inner + lax.rem(
            minor + step_minor + inner, inner
        )

    return outer, at


def greet(axes):
    barrier = pltpu.get_barrier_semaphore()
    greeted = 0
    for axis, inner in axes:
        outer, at = place(axis, inner)
        steps = [(d, 0) for d in range(1, outer)] + [(0, e) for e in range(1, inner)]
        for d, e in steps:
            pl.semaphore_signal(
                barrier, inc=1, device_id=target(axis, at(d, e)), device_id_type=MESH
            )
            greeted += 1
    pl.semaphore_wait(barrier, greeted)


def remote(source, landing, sems, slot, axis, index):
    return pltpu.make_async_remote_copy(
        src_ref=source,
        dst_ref=landing,
        send_sem=sems[0].at[slot],
        recv_sem=sems[1].at[slot],
        device_id=target(axis, index),
        device_id_type=MESH,
    )


class Gather:
    def __init__(self, axis, inner, part, sems, base=0):
        self.axis, self.inner, self.part, self.sems, self.base = axis, inner, part, sems, base
        self.outer, self.at = place(axis, inner)
        self.started = []

    def copy(self, block, d, e, index):
        return remote(block, block, self.sems, self.base + e * self.outer + d, self.axis, index)

    def start(self):
        own = self.part(self.at(0, 0))
        for d in range(1, self.outer):
            self.started.append(self.copy(own, d, 0, self.at(d, 0)))
            self.started[-1].start()
        for e in range(1, self.inner):
            self.started.append(self.copy(own, 0, e, self.at(0, e)))
            self.started[-1].start()

    def forward(self):
        for d in range(1, self.outer):
            landed = self.part(self.at(-d, 0))
            self.copy(landed, d, 0, self.at(d, 0)).wait_recv()
            for e in range(1, self.inner):
                self.started.append(self.copy(landed, d, e, self.at(0, e)))
                self.started[-1].start()

    def finish(self):
        for e in range(1, self.inner):
            for d in range(self.outer):
                self.copy(self.part(self.at(-d, -e)), d, e, self.at(0, e)).wait_recv()

    def drain(self):
        for copy in self.started:
            copy.wait_send()


class SumScatter:
    def __init__(self, axis, inner, part, near, staged, far, sems, base=0):
        self.axis, self.inner, self.part = axis, inner, part
        self.near, self.staged, self.far = near, staged, far
        self.sems, self.base = sems, base
        self.outer, self.at = place(axis, inner)
        self.order = list(range(1, self.outer)) + [0]
        self.started = []

    def near_copy(self, d, e):
        return remote(
            self.part(self.at(d, e)),
            self.near.at[(e - 1) * self.outer + d],
            self.sems,
            self.base + e * self.outer + d,
            self.axis,
            self.at(0, e),
        )

    def far_copy(self, d):
        return remote(
            self.staged.at[d - 1],
            self.far.at[d - 1],
            self.sems,
            self.base + d,
            self.axis,
            self.at(d, 0),
        )

    def start(self, produce):
        for d in self.order:
            for e in range(1, self.inner):
                produce(self.at(d, e))
                self.started.append(self.near_copy(d, e))
                self.started[-1].start()
        for d in self.order:
            produce(self.at(d, 0))

    def forward(self):
        for d in self.order:
            total = self.part(self.at(d, 0))[...].astype(jnp.float32)
            for e in range(1, self.inner):
                self.near_copy(d, e).wait_recv()
                total = total + self.near[(e - 1) * self.outer + d].astype(jnp.float32)
            if d:
                self.staged[d - 1] = total.astype(jnp.bfloat16)
                self.started.append(self.far_copy(d))
                self.started[-1].start()
        self.total = total

    def finish(self):
        total = self.total
        for d in range(1, self.outer):
            self.far_copy(d).wait_recv()
            total = total + self.far[d - 1].astype(jnp.float32)
        return total.astype(jnp.bfloat16)

    def drain(self):
        for copy in self.started:
            copy.wait_send()


def tiles(width):
    step = 256 if width % 256 == 0 else width
    return width // step, step


CHUNK_HEADS = 4
OUT_PARTS = 2


def kernel(
    req_inner,
    core_inner,
    chunks,
    hidden_ref,
    rotary_ref,
    block_live_ref,
    parent_ref,
    size_ref,
    owner_ref,
    wq_ref,
    wkv_ref,
    cache_ref,
    wo_ref,
    out_ref,
    rows,
    wq,
    wkv,
    wo,
    cache,
    kv_all,
    slots,
    mixed_rows,
    pick_ref,
    unpick_ref,
    live_ref,
    load_sem,
    row_send,
    row_recv,
    cache_send,
    cache_recv,
    sum_send,
    sum_recv,
    kv_send,
    kv_recv,
    slot_send,
    slot_recv,
    out_send,
    out_recv,
    *buffers,
):
    tensor_count, req_count = lax.axis_size("tensor"), lax.axis_size("req")
    me, slot = lax.axis_index("tensor"), lax.axis_index("req")
    rows_here = hidden_ref.shape[0]
    query_columns = wq.shape[1]
    heads_here = query_columns // HEAD_SIZE
    group_size = QUERY_HEADS // KEYVALUE_HEADS
    pair = 2 * HEAD_SIZE
    positions = cache_ref.shape[0]
    chunk_width = query_columns // chunks
    chunk_heads = chunk_width // HEAD_SIZE
    score_scale = 1.0 / math.sqrt(HEAD_SIZE)
    loads = [
        pltpu.make_async_copy(source, landing, load_sem.at[i])
        for i, (source, landing) in enumerate(((wkv_ref, wkv), (wq_ref, wq), (wo_ref, wo)))
    ]
    for load in loads:
        load.start()
    greet([("tensor", tensor_count), ("req", req_inner)])

    def row_span(index):
        return pl.ds(pl.multiple_of(index * rows_here, rows_here), rows_here)

    def slot_span(index):
        return pl.ds(pl.multiple_of(index * MOST_TREE_NODES, MOST_TREE_NODES), MOST_TREE_NODES)

    rows[row_span(me), :] = hidden_ref[...]
    row_gather = Gather(
        "tensor", core_inner, lambda index: rows.at[row_span(index)], (row_send, row_recv)
    )
    row_gather.start()

    def cache_part(owner, reader):
        head = reader * heads_here // group_size
        return (
            cache_ref.at[:, pl.ds(pl.multiple_of(head * pair, pair), pair)],
            cache.at[pl.ds(pl.multiple_of(owner * positions, positions), positions)],
        )

    own_cache = pltpu.make_async_copy(*cache_part(me, me), load_sem.at[3])
    own_cache.start()
    cache_sems = (cache_send, cache_recv)
    cache_copies = []
    for step in range(1, tensor_count):
        reader = lax.rem(me + step, tensor_count)
        copy = remote(*cache_part(me, reader), cache_sems, step, "tensor", reader)
        copy.start()
        cache_copies.append(copy)

    requests = size_ref.shape[0]
    sizes = [size_ref[r] for r in range(requests)]
    owners = [owner_ref[s] for s in range(requests)]
    slot_sizes, slot_starts = [], []
    for owner in owners:
        size, start = jnp.int32(0), jnp.int32(0)
        for r in range(requests):
            size = size + jnp.where(owner == r, sizes[r], 0)
            start = start + jnp.where(owner > r, sizes[r], 0)
        slot_sizes.append(size)
        slot_starts.append(start)
    row_total = rows.shape[0]
    block_shape = (MOST_TREE_NODES, row_total)
    block_nodes = lax.broadcasted_iota(jnp.int32, block_shape, 0)
    block_lag = lax.broadcasted_iota(jnp.int32, block_shape, 1) - block_nodes
    for s in range(requests):
        pick_ref[s * MOST_TREE_NODES : (s + 1) * MOST_TREE_NODES, :] = jnp.where(
            (block_lag == slot_starts[s]) & (block_nodes < slot_sizes[s]), 1.0, 0.0
        ).astype(jnp.bfloat16)
    row_gather.forward()
    row_gather.finish()

    scatters = []
    for c in range(chunks + 1):
        product, blocks, near, staged, far = buffers[5 * c : 5 * c + 5]
        if c == 0:
            loads[0].wait()
            product[...] = jnp.dot(
                rows[...], wkv[...], preferred_element_type=jnp.float32
            ).astype(jnp.bfloat16)
        else:
            if c == 1:
                loads[1].wait()
            product[...] = jnp.dot(
                rows[...],
                wq[:, (c - 1) * chunk_width : c * chunk_width],
                preferred_element_type=jnp.float32,
            ).astype(jnp.bfloat16)

        def produce(index, blocks=blocks, product=product):
            blocks[slot_span(index), :] = jnp.dot(
                pick_ref[slot_span(index), :], product[...], preferred_element_type=jnp.float32
            ).astype(jnp.bfloat16)

        scatter = SumScatter(
            "req",
            req_inner,
            lambda index, blocks=blocks: blocks.at[slot_span(index)],
            near,
            staged,
            far,
            (sum_send, sum_recv),
            c * req_count,
        )
        scatter.start(produce)
        scatters.append(scatter)

    unpick_shape = unpick_ref.shape
    slot_columns = lax.broadcasted_iota(jnp.int32, (1, unpick_shape[1]), 1)
    lag = jnp.full((1, unpick_shape[1]), -unpick_shape[0] - unpick_shape[1], jnp.int32)
    for s in range(requests):
        nodes = slot_columns - s * MOST_TREE_NODES
        inside = (nodes >= 0) & (nodes < slot_sizes[s])
        lag = jnp.where(inside, slot_starts[s] - s * MOST_TREE_NODES, lag)
    unpick_lag = lax.broadcasted_iota(
        jnp.int32, unpick_shape, 0
    ) - lax.broadcasted_iota(jnp.int32, unpick_shape, 1)
    unpick_ref[...] = jnp.where(unpick_lag == lag, 1.0, 0.0).astype(jnp.bfloat16)

    scatters[0].forward()
    tile = 1024
    block_live = jnp.where(block_live_ref[...] > 0, 1.0, 0.0).astype(jnp.bfloat16)
    block_live = jnp.broadcast_to(block_live, (16, block_live.shape[1]))

    @pl.loop(0, cache.shape[0] // tile)
    def _(i):
        shape = (block_live.shape[1], tile)
        offset = (
            lax.broadcasted_iota(jnp.int32, shape, 1)
            + i * tile
            - lax.broadcasted_iota(jnp.int32, shape, 0) * CBLK
        )
        spread = jnp.where((offset >= 0) & (offset < CBLK), 1.0, 0.0).astype(jnp.bfloat16)
        alive = jnp.dot(block_live, spread, preferred_element_type=jnp.float32)
        live_ref[:, pl.ds(pl.multiple_of(i * tile, tile), tile)] = jnp.where(
            alive[:1] > 0.5, 0.0, NEGATIVE
        )

    square = (MOST_TREE_NODES, MOST_TREE_NODES)
    node_rows = lax.broadcasted_iota(jnp.int32, square, 0)
    node_columns = lax.broadcasted_iota(jnp.int32, square, 1)
    parents = parent_ref[pl.ds(owner_ref[slot], 1), :].astype(jnp.float32)
    parents = jnp.sum(
        jnp.where(node_rows == node_columns, parents, 0.0), axis=1, keepdims=True
    ).astype(jnp.int32)
    closure = jnp.where((node_rows == node_columns) | (node_columns == parents), 1.0, 0.0)
    for sweep in range((MOST_TREE_NODES - 1).bit_length()):
        link = closure.astype(jnp.bfloat16)
        closure = jnp.minimum(jnp.dot(link, link, preferred_element_type=jnp.float32), 1.0)
    depth = jnp.sum(closure, axis=1, keepdims=True).astype(jnp.int32) - 1
    at_depth = jnp.where(node_columns == depth, 1.0, 0.0)
    rotary = jnp.dot(
        at_depth,
        rotary_ref[...],
        preferred_element_type=jnp.float32,
        precision=lax.Precision.HIGHEST,
    )
    cosine, sine = rotary[:, :HEAD_SIZE], rotary[:, HEAD_SIZE:]
    tree_bias = jnp.where(closure > 0.5, 0.0, NEGATIVE)
    tree_bias = jnp.concatenate([tree_bias] * chunk_heads, axis=0)
    scatters[1].forward()
    kv_all[me] = scatters[0].finish()
    kv_gather = Gather(
        "tensor", tensor_count, lambda index: kv_all.at[index], (kv_send, kv_recv)
    )
    kv_gather.start()

    def rotated(values):
        widened = values.astype(jnp.float32)
        turned = jnp.concatenate(
            [widened[:, HEAD_SIZE // 2 :], widened[:, : HEAD_SIZE // 2]], axis=1
        )
        return (widened * cosine + turned * sine).astype(jnp.bfloat16)

    for c in range(2, min(chunks, 3) + 1):
        scatters[c].forward()
    kv_gather.finish()
    kv_head = me * heads_here // group_size
    kv_columns = kv_all.shape[2]
    source_ids = lax.broadcasted_iota(jnp.int32, (kv_columns, pair), 0)
    wanted_ids = lax.broadcasted_iota(jnp.int32, (kv_columns, pair), 1) * KEYVALUE_HEADS + kv_head
    head_kv = jnp.zeros((MOST_TREE_NODES, pair), jnp.float32)
    for t in range(tensor_count):
        chosen = jnp.where(source_ids + t * kv_columns == wanted_ids, 1.0, 0.0)
        head_kv = head_kv + jnp.dot(
            kv_all[t], chosen.astype(jnp.bfloat16), preferred_element_type=jnp.float32
        )
    tree_key = rotated(head_kv[:, :HEAD_SIZE])
    tree_value = head_kv[:, HEAD_SIZE:].astype(jnp.bfloat16)
    own_cache.wait()
    for step in range(1, tensor_count):
        owner = lax.rem(me - step + tensor_count, tensor_count)
        remote(*cache_part(owner, me), cache_sems, step, "tensor", owner).wait_recv()

    def scored(query, key):
        return (
            lax.dot_general(
                query, key, (((1,), (1,)), ((), ())), preferred_element_type=jnp.float32
            )
            * score_scale
        )

    gathers = []
    for c in range(chunks):
        found = scatters[c + 1].finish()
        query = jnp.concatenate(
            [rotated(found[:, h * HEAD_SIZE : (h + 1) * HEAD_SIZE]) for h in range(chunk_heads)],
            axis=0,
        )
        scores = scored(query, tree_key) + tree_bias
        top = jnp.max(scores, axis=1, keepdims=True)
        weights = jnp.exp(scores - top)
        total = jnp.sum(weights, axis=1, keepdims=True)
        mix = jnp.dot(
            weights.astype(jnp.bfloat16), tree_value, preferred_element_type=jnp.float32
        )

        def step_tile(i, carry, query=query):
            top, total, mix = carry
            span = pl.ds(pl.multiple_of(i * tile, tile), tile)
            scores = scored(query, cache[span, :HEAD_SIZE]) + live_ref[:, span]
            higher = jnp.maximum(top, jnp.max(scores, axis=1, keepdims=True))
            scale = jnp.exp(top - higher)
            weights = jnp.exp(scores - higher)
            total = total * scale + jnp.sum(weights, axis=1, keepdims=True)
            mix = mix * scale + jnp.dot(
                weights.astype(jnp.bfloat16),
                cache[span, HEAD_SIZE:],
                preferred_element_type=jnp.float32,
            )
            return higher, total, mix

        top, total, mix = lax.fori_loop(
            0, cache.shape[0] // tile, step_tile, (top, total, mix)
        )
        mix = (mix / total).astype(jnp.bfloat16)
        for h in range(chunk_heads):
            low = c * chunk_width + h * HEAD_SIZE
            slots[slot_span(slot), low : low + HEAD_SIZE] = mix[
                h * MOST_TREE_NODES : (h + 1) * MOST_TREE_NODES
            ]
        gather = Gather(
            "req",
            req_inner,
            lambda index, c=c: slots.at[
                slot_span(index), c * chunk_width : (c + 1) * chunk_width
            ],
            (slot_send, slot_recv),
            c * req_count,
        )
        gather.start()
        if c + 3 < chunks:
            scatters[c + 4].forward()
        if gathers:
            gathers[-1].forward()
        gathers.append(gather)
    gathers[-1].forward()
    for c, gather in enumerate(gathers):
        gather.finish()
        columns = slice(c * chunk_width, (c + 1) * chunk_width)
        mixed_rows[:, columns] = jnp.dot(
            unpick_ref[...], slots[:, columns], preferred_element_type=jnp.float32
        ).astype(jnp.bfloat16)

    loads[2].wait()
    out_width = wo.shape[1] // OUT_PARTS
    out_sums = []
    for p in range(OUT_PARTS):
        product, near, staged, far = buffers[5 * (chunks + 1) + 4 * p :][:4]
        steps, step_width = tiles(out_width)

        @pl.loop(0, steps)
        def _(step, p=p, product=product):
            columns = pl.ds(pl.multiple_of(step * step_width, step_width), step_width)
            wide = pl.ds(
                pl.multiple_of(p * out_width + step * step_width, step_width), step_width
            )
            product[:, columns] = jnp.dot(
                mixed_rows[...], wo[:, wide], preferred_element_type=jnp.float32
            ).astype(jnp.bfloat16)

        out_sum = SumScatter(
            "tensor",
            core_inner,
            lambda index, product=product: product.at[row_span(index)],
            near,
            staged,
            far,
            (out_send, out_recv),
            p * tensor_count,
        )
        out_sum.start(lambda index: None)
        out_sums.append(out_sum)
    for out_sum in out_sums:
        out_sum.forward()
    for p, out_sum in enumerate(out_sums):
        out_ref[:, p * out_width : (p + 1) * out_width] = out_sum.finish()
    for work in [row_gather, kv_gather] + scatters + gathers + out_sums:
        work.drain()
    for copy in cache_copies:
        copy.wait_send()


def run(hidden, tables, w_query, keyvalue_weight, cache, w_out):
    tensor_count, req_count = lax.axis_size("tensor"), lax.axis_size("req")
    req_inner, core_inner = inner_of(req_count), 2
    rows_here, width = hidden.shape
    row_total = rows_here * tensor_count
    query_columns, kv_columns = w_query.shape[1], keyvalue_weight.shape[1]
    chunks = query_columns // HEAD_SIZE // CHUNK_HEADS
    depth, out_columns = w_out.shape
    bf16, dma = jnp.bfloat16, pltpu.SemaphoreType.DMA
    any_space, vmem = pl.BlockSpec(memory_space=pl.ANY), pl.BlockSpec(memory_space=pltpu.VMEM)
    outer, core_outer = req_count // req_inner, tensor_count // core_inner
    buffers = []
    for columns in [kv_columns] + [query_columns // chunks] * chunks:
        buffers += [
            pltpu.VMEM((row_total, columns), bf16),
            pltpu.VMEM((req_count * MOST_TREE_NODES, columns), bf16),
            pltpu.VMEM(((req_inner - 1) * outer, MOST_TREE_NODES, columns), bf16),
            pltpu.VMEM((outer - 1, MOST_TREE_NODES, columns), bf16),
            pltpu.VMEM((outer - 1, MOST_TREE_NODES, columns), bf16),
        ]
    for part in range(OUT_PARTS):
        columns = out_columns // OUT_PARTS
        buffers += [
            pltpu.VMEM((row_total, columns), bf16),
            pltpu.VMEM(((core_inner - 1) * core_outer, rows_here, columns), bf16),
            pltpu.VMEM((core_outer - 1, rows_here, columns), bf16),
            pltpu.VMEM((core_outer - 1, rows_here, columns), bf16),
        ]
    sems = [tensor_count, tensor_count, (chunks + 1) * req_count, tensor_count]
    sems += [chunks * req_count, OUT_PARTS * tensor_count]
    return pl.pallas_call(
        functools.partial(kernel, req_inner, core_inner, chunks),
        out_shape=jax.ShapeDtypeStruct((rows_here, out_columns), bf16),
        in_specs=[vmem] * 4 + [pl.BlockSpec(memory_space=pltpu.SMEM)] * 2 + [any_space] * 4,
        out_specs=vmem,
        scratch_shapes=[
            pltpu.VMEM((row_total, width), bf16),
            pltpu.VMEM(w_query.shape, bf16),
            pltpu.VMEM(keyvalue_weight.shape, bf16),
            pltpu.VMEM(w_out.shape, bf16),
            pltpu.VMEM((cache.shape[0] * tensor_count, 2 * HEAD_SIZE), bf16),
            pltpu.VMEM((tensor_count, MOST_TREE_NODES, kv_columns), bf16),
            pltpu.VMEM((req_count * MOST_TREE_NODES, depth), bf16),
            pltpu.VMEM((row_total, depth), bf16),
            pltpu.VMEM((req_count * MOST_TREE_NODES, row_total), bf16),
            pltpu.VMEM((row_total, req_count * MOST_TREE_NODES), bf16),
            pltpu.VMEM((1, CACHE_POSITIONS), jnp.float32),
            dma((4,)),
        ]
        + [dma((count,)) for count in sems for both in range(2)]
        + buffers,
        compiler_params=pltpu.CompilerParams(
            collective_id=0, has_side_effects=True, vmem_limit_bytes=VMEM_BYTES
        ),
    )(hidden, *tables, w_query, keyvalue_weight, cache, w_out)


def body(
    hidden,
    w_query,
    keyvalue_weight,
    w_out,
    keyvalue_cache,
    cache_live,
    tree_size,
    tree_parent,
    slot_request,
):
    tables = (rotary_tables(), cache_live, tree_parent, tree_size, slot_request)
    return run(hidden, tables, w_query, keyvalue_weight, keyvalue_cache[0], w_out)


def solution(mesh):
    placed = (
        P("tensor", "req"),
        P("req", "tensor"),
        P("req", "tensor"),
        P("tensor", "req"),
        P("req", "tensor", None),
        P("req", None),
        P(),
        P(),
        P(),
    )
    return jax.shard_map(
        body, mesh=mesh, in_specs=placed, out_specs=P("tensor", "req"), check_vma=False
    )
```
